256 devices in a mesh: section: 8 (over y, core), seq: 32 (over x, z).
Axes of the slice: x: 4, y: 4, z: 8, core: 2. Of those that a mesh axis runs over, the one named last changes fastest.
Arguments:
- query: bfloat16 [8, 8192, 3072], P('section', 'seq'), may hold values from -60 to 60
- keys: bfloat16 [8, 8192, 1024], P('section', 'seq'), may hold values from -6 to 6
- values: bfloat16 [8, 8192, 1024], P('section', 'seq'), may hold values from -6 to 6
- documents: int32 [8, 64], P('section'), may hold values from 0 to 7, never falling along the last dimension, each value on 1 to 48 neighbouring positions
- retrieval_heads: int32 [8, 2], P('section'), may hold values from 0 to 7, as said below
Outputs:
- next_input: bfloat16 [8, 8192, 3072], P('section', 'seq')
The draws below stay inside these ranges and needn't reach their ends.
Inputs may be any that keep to these rules, and one draw needn't show every extreme that they name: `documents`: document numbers never fall along a group; every document 0 to 7 occupies 1 to 48 consecutive blocks, and one occupies exactly 48. `retrieval_heads`: each section lists 2 different key and value heads.
All inputs are finite; a program needn't handle non-finite values.
Results may differ from the reference program's by a relative error of at most 0.0041.
Values may be sent and summed in bfloat16 or wider, within the bound.
A program may use at most 128 MiB of HBM per device.

```python
import math
import jax
import jax.numpy as jnp
import numpy as np
from jax import lax

KVH = 8
HEAD_SIZE = 128
RKV = 2
BLK = 128
WBLOCKS = 8
TOK_DEV = 256
GQ = 3
SECTIONS = 8
GROUP = 8192
NB = 64
DOCS = 8
MOST_BLOCKS = 48
N_SEQ = 32


def query_key_pair(key):
    base = jax.random.fold_in(key, 11)
    key_q, key_k = jax.random.split(base, 2)
    keys_all = jax.random.truncated_normal(key_k, -6.0, 6.0, (SECTIONS, GROUP, KVH, HEAD_SIZE), jnp.float32)
    query_all = jax.random.truncated_normal(key_q, -6.0, 6.0, (SECTIONS, GROUP, KVH, GQ, HEAD_SIZE), jnp.float32)
    return (query_all.reshape(SECTIONS, GROUP, KVH * GQ * HEAD_SIZE), keys_all.reshape(SECTIONS, GROUP, KVH * HEAD_SIZE))


def draw_query(key, part):
    return query_key_pair(key)[0].astype(jnp.bfloat16)


def draw_keys(key, part):
    return query_key_pair(key)[1].astype(jnp.bfloat16)


def draw_retrieval_heads(key, part):
    section_keys = jax.random.split(jax.random.fold_in(key, 23), SECTIONS)
    picks = jax.vmap(lambda one: jax.random.permutation(one, KVH)[:RKV])(section_keys)
    return picks.astype(jnp.int32)


def levels(key, shape, cuts, low, largest):
    level, own = 1.0, jax.random.fold_in(key, 6)
    for position, parts in cuts:
        steps = jnp.exp(jax.random.uniform(jax.random.fold_in(own, position), (parts,), jnp.float32, low / len(cuts), largest / len(cuts)))
        level = level * jnp.repeat(steps, shape[position] // parts).reshape([-1 if axis == position else 1 for axis in range(len(shape))])
    return level


def length_profile(number_of, total, most, skew):
    portions = [(1 << 20) // math.isqrt(rank ** skew) + 1 for rank in range(2, number_of + 1)]
    surplus, holding = total - most - (number_of - 1), [1] * (number_of - 1)
    while surplus > 0:
        movable = [i for i in range(number_of - 1) if holding[i] < most]
        whole, remaining = sum([portions[i] for i in movable]), surplus
        for i in movable:
            addition = min(most - holding[i], max(1, remaining * portions[i] // whole), surplus)
            holding[i] = holding[i] + addition
            surplus = surplus - addition
    return np.array([most] + holding)


def ragged_sizes(key, number_of, total, bound, slope):
    if number_of == 2:
        one = jax.random.randint(key, (), max(1, total - bound), min(bound, total - 1) + 1)
        return jnp.stack([one, total - one])
    tallies = jnp.asarray(length_profile(number_of, total, bound, slope), jnp.int32)
    twos = (number_of - 1) // 2
    source_of, sink = tallies[1:1 + 2 * twos:2], tallies[2:2 + 2 * twos:2]
    room = jnp.minimum(source_of - 1, bound - sink)
    passed = jax.random.randint(jax.random.fold_in(key, 1), (twos,), 0, 1 << 20) % (room + 1)
    tallies = tallies.at[1:1 + 2 * twos:2].set(source_of - passed).at[2:2 + 2 * twos:2].set(sink + passed)
    return tallies[jax.random.permutation(jax.random.fold_in(key, 2), number_of)]


def centred(stream_key, extent, spread, reach, shards=(), held_as=jnp.bfloat16):
    array = spread * jax.random.normal(stream_key, extent, jnp.float32)
    if shards:
        array = array * levels(stream_key, extent, shards, -0.22, 0.18)
    return jnp.clip(array, -reach, reach).astype(held_as)


def setup_inputs(seed: int = 0) -> dict:
    splits = jax.random.split(jax.random.key(seed), 6)
    return {
        "query": draw_query(jax.random.fold_in(splits[5], 71), 0),
        "keys": draw_keys(jax.random.fold_in(splits[5], 71), 0),
        "values": centred(splits[2], (SECTIONS, GROUP, KVH * HEAD_SIZE), 1.0, 6.0, ((0, 8), (1, 32))),
        "documents": jax.vmap(lambda own: jnp.searchsorted(jnp.cumsum(ragged_sizes(own, DOCS, NB, MOST_BLOCKS, 2)), jnp.arange(NB), side="right"))(jax.random.split(splits[3], SECTIONS)).reshape((SECTIONS, NB)).astype(jnp.int32),
        "retrieval_heads": draw_retrieval_heads(jax.random.fold_in(splits[5], 71), 0),
    }


def masked_softmax_values(score, allow, vals):
    score = jnp.where(allow, score, -1e+30)
    top = lax.optimization_barrier(jnp.max(score, axis=-1, keepdims=True))
    weight = jnp.where(allow, jnp.exp(score - top), 0.0)
    total = lax.optimization_barrier(jnp.sum(weight, axis=-1))
    low = weight.astype(jnp.bfloat16)
    low = lax.optimization_barrier(low).astype(jnp.float32)
    mixed = jnp.einsum('jqk,kd->qjd', low, vals)
    return (mixed / jnp.transpose(total)[:, :, None]).astype(jnp.bfloat16)

def section_attention(query_s, keys_s, values_s, doc_row, heads_row):
    length = query_s.shape[0]
    qr = query_s.reshape(length, KVH, GQ, HEAD_SIZE).astype(jnp.float32)
    kr = keys_s.reshape(length, KVH, HEAD_SIZE).astype(jnp.float32)
    vr = values_s.reshape(length, KVH, HEAD_SIZE).astype(jnp.float32)
    pos = jnp.arange(length, dtype=jnp.int32)
    doc = doc_row[pos // BLK]
    scale = 1.0 / math.sqrt(HEAD_SIZE)
    query_block_rows = min(512, length)
    n_blocks = length // query_block_rows
    padded_window = (WBLOCKS - 1) * BLK
    chosen = jnp.any(heads_row[:, None] == jnp.arange(KVH, dtype=jnp.int32)[None, :], axis=0)

    def retrieval_head(index_value):
        kg = lax.dynamic_index_in_dim(kr, index_value, 1, keepdims=False)
        value_group = lax.dynamic_index_in_dim(vr, index_value, 1, keepdims=False)
        qg = lax.dynamic_index_in_dim(qr, index_value, 1, keepdims=False)

        def one_block(block):
            query_slices = (block * query_block_rows).astype(jnp.int32)
            qblk = lax.dynamic_slice_in_dim(qg, query_slices, query_block_rows, 0)
            qpos = query_slices + jnp.arange(query_block_rows, dtype=jnp.int32)
            qdoc = lax.dynamic_slice_in_dim(doc, query_slices, query_block_rows, 0)
            score = jnp.einsum('qjd,kd->jqk', qblk, kg) * scale
            allow = (pos[None, :] <= qpos[:, None]) & (doc[None, :] == qdoc[:, None])
            return masked_softmax_values(score, allow[None], value_group)
        outs = lax.map(one_block, jnp.arange(n_blocks, dtype=jnp.int32))
        return outs.reshape(length, GQ, HEAD_SIZE)

    def running_head(index_value):
        kg = lax.dynamic_index_in_dim(kr, index_value, 1, keepdims=False)
        value_group = lax.dynamic_index_in_dim(vr, index_value, 1, keepdims=False)
        qg = lax.dynamic_index_in_dim(qr, index_value, 1, keepdims=False)
        kpad = jnp.concatenate([jnp.zeros((padded_window, HEAD_SIZE), kg.dtype), kg], axis=0)
        padded_values = jnp.concatenate([jnp.zeros((padded_window, HEAD_SIZE), value_group.dtype), value_group], axis=0)
        spos = jnp.arange(BLK, dtype=jnp.int32)

        def one_block(block):
            query_slices = (block * query_block_rows).astype(jnp.int32)
            qblk = lax.dynamic_slice_in_dim(qg, query_slices, query_block_rows, 0)
            qpos = query_slices + jnp.arange(query_block_rows, dtype=jnp.int32)
            wk = lax.dynamic_slice_in_dim(kpad, query_slices, padded_window + query_block_rows, 0)
            value_weight = lax.dynamic_slice_in_dim(padded_values, query_slices, padded_window + query_block_rows, 0)
            wpos = query_slices - padded_window + jnp.arange(padded_window + query_block_rows, dtype=jnp.int32)
            allow_w = (wpos[None, :] >= 0) & (wpos[None, :] <= qpos[:, None]) & (qpos[:, None] // BLK - wpos[None, :] // BLK < WBLOCKS)
            allow_s = (qpos[:, None] // BLK >= WBLOCKS) & (spos[None, :] >= 0)
            allk = jnp.concatenate([kg[:BLK], wk], axis=0)
            allv = jnp.concatenate([value_group[:BLK], value_weight], axis=0)
            allow = jnp.concatenate([allow_s, allow_w], axis=1)
            score = jnp.einsum('qjd,kd->jqk', qblk, allk) * scale
            return masked_softmax_values(score, allow[None], allv)
        outs = lax.map(one_block, jnp.arange(n_blocks, dtype=jnp.int32))
        return outs.reshape(length, GQ, HEAD_SIZE)

    def one_head(index_value):
        return lax.cond(chosen[index_value], retrieval_head, running_head, index_value)
    heads_out = lax.map(one_head, jnp.arange(KVH, dtype=jnp.int32))
    return jnp.transpose(heads_out, (1, 0, 2, 3)).reshape(length, KVH * GQ * HEAD_SIZE)

def reference(query, keys, values, documents, retrieval_heads):
    half_rows = TOK_DEV // 2
    rows = jnp.arange(GROUP, dtype=jnp.int32)
    position_of_row = (rows % TOK_DEV // half_rows * N_SEQ + rows // TOK_DEV) * half_rows + rows % half_rows
    run_index = rows // half_rows
    row_of_position = run_index % N_SEQ * TOK_DEV + run_index // N_SEQ * half_rows + rows % half_rows
    query_p = jnp.take(query, row_of_position.astype(jnp.int32), axis=1)
    keys_p = jnp.take(keys, row_of_position.astype(jnp.int32), axis=1)
    values_p = jnp.take(values, row_of_position.astype(jnp.int32), axis=1)

    def per_section(items):
        return section_attention(items[0], items[1], items[2], items[3], items[4])
    results = lax.map(per_section, (query_p, keys_p, values_p, documents, retrieval_heads))
    results = jnp.take(results, position_of_row.astype(jnp.int32), axis=1)
    return jnp.roll(results, 1, axis=0)
```

```python
import math

import jax
import jax.numpy as jnp
from jax import lax
from jax.experimental import pallas as pl
from jax.experimental.pallas import tpu as pltpu
from jax.sharding import PartitionSpec as P

KVH = 8
HEAD_SIZE = 128
RKV = 2
BLK = 128
WBLOCKS = 8
RUN = KVH - RKV
GQ = 3
ROWS = GQ * BLK
NZ = 8
NX = 4
LEAD = 2
NEG = -1e30
LOW = -1e29
CEXP = math.log2(math.e) / math.sqrt(HEAD_SIZE)
MESH = pl.DeviceIdType.MESH


def dot_nt(a, b):
    return lax.dot_general(a, b, (((1,), (1,)), ((), ())), preferred_element_type=jnp.float32)


def kernel(
    docs, heads, q_ref, k_ref, v_ref, out_ref,
    kv, sink, qx, po, pr, st, sr, res, outst, s_ref,
    ksend, krecv, ssend, srecv, qsend, qrecv, psend, precv, tsend, trecv, osend, orecv,
):
    sec = lax.axis_index("section")
    me = lax.axis_index("seq")
    nsec = lax.axis_size("section")
    nseq = NX * NZ
    x, z = me // NZ, me % NZ
    lo = jnp.minimum(heads[0, 0], heads[0, 1])
    hi = jnp.maximum(heads[0, 0], heads[0, 1])

    row_next, row_prev = x * NZ + (z + 1) % NZ, x * NZ + (z + NZ - 1) % NZ
    pos_next, pos_prev = (me + 1) % nseq, (me + nseq - 1) % nseq
    pos_far, pos_back = (me + NZ - 1) % nseq, (me + nseq - NZ + 1) % nseq
    wrap_next = (me + 1) // nseq
    wrap_prev = 1 - (me + nseq - 1) // nseq
    wrap_far = (me + NZ - 1) // nseq

    def peer(c, kind):
        ret = c < RKV
        if kind == "next":
            return jnp.where(ret, row_next, pos_next), jnp.where(ret, 0, wrap_next)
        if kind == "prev":
            return jnp.where(ret, row_prev, pos_prev), jnp.where(ret, 0, wrap_prev)
        return jnp.where(ret, row_prev, pos_far), jnp.where(ret, 0, wrap_far)

    def block_copy(c, half, src, dh, dst, to):
        return pltpu.make_async_remote_copy(
            src_ref=kv.at[c, half, :, src], dst_ref=kv.at[c, dh, :, dst],
            send_sem=ksend.at[c, dst, half], recv_sem=krecv.at[c, dst, dh],
            device_id={"seq": to}, device_id_type=MESH,
        )

    def push(c, src, dst, kind):
        to, swap = peer(c, kind)
        for half in range(2):
            dh = swap if half == 0 else 1 - swap
            block_copy(c, half, src, dh, dst, to).start()

    def landed(c, slot):
        for half in range(2):
            block_copy(c, half, slot, half, slot, pos_next).wait_recv()
        if slot:
            give_sink(c, slot)

    def sink_copy(c, slot, r):
        return pltpu.make_async_remote_copy(
            src_ref=kv.at[c, 0, :, slot], dst_ref=sink.at[c - RKV],
            send_sem=ssend.at[c - RKV, r - 1], recv_sem=srecv.at[c - RKV],
            device_id={"seq": r * NZ + z}, device_id_type=MESH,
        )

    def give_sink(c, slot):
        @pl.when((x == 0) & (z == slot) & (c >= RKV))
        def _():
            for r in range(1, NX):
                sink_copy(c, slot, r).start()

    def q_copy(e):
        return pltpu.make_async_remote_copy(
            src_ref=qx.at[0], dst_ref=qx.at[e], send_sem=qsend.at[e - 1], recv_sem=qrecv.at[e - 1],
            device_id={"seq": (x + e) % NX * NZ + z}, device_id_type=MESH,
        )

    def part_copies(e, h):
        to = (x + NX - e) % NX * NZ + z
        return (
            pltpu.make_async_remote_copy(
                src_ref=po.at[e, h], dst_ref=pr.at[e - 1, h],
                send_sem=psend.at[e - 1, h], recv_sem=precv.at[e - 1, h],
                device_id={"seq": to}, device_id_type=MESH,
            ),
            pltpu.make_async_remote_copy(
                src_ref=st.at[e, h], dst_ref=sr.at[e - 1, h],
                send_sem=tsend.at[e - 1, h], recv_sem=trecv.at[e - 1, h],
                device_id={"seq": to}, device_id_type=MESH,
            ),
        )

    def out_copy(k):
        return pltpu.make_async_remote_copy(
            src_ref=outst.at[k], dst_ref=out_ref.at[:, pl.ds(pl.multiple_of(k * ROWS, 128), ROWS)],
            send_sem=osend.at[k], recv_sem=orecv.at[k],
            device_id={"section": (sec + 1) % nsec}, device_id_type=MESH,
        )

    def head_of(c):
        k = c - RKV
        g = k + (k >= lo).astype(jnp.int32)
        g = g + (g >= hi).astype(jnp.int32)
        return jnp.where(c == 0, heads[0, 0], jnp.where(c == 1, heads[0, 1], g))

    def place_of(g):
        run = RKV + g - (g > lo).astype(jnp.int32) - (g > hi).astype(jnp.int32)
        return jnp.where(g == heads[0, 0], 0, jnp.where(g == heads[0, 1], 1, run))

    barrier = pltpu.get_barrier_semaphore()
    near = [row_next, row_prev, pos_next, pos_prev, pos_far, pos_back]
    near += [(x + e) % NX * NZ + z for e in range(1, NX)]
    for to in near:
        pl.semaphore_signal(barrier, inc=1, device_id={"seq": to}, device_id_type=MESH)
    for by in (1, nsec - 1):
        pl.semaphore_signal(
            barrier, inc=1, device_id={"section": (sec + by) % nsec}, device_id_type=MESH
        )

    def columns(ref, half, g, width):
        rows = pl.ds(pl.multiple_of(half * BLK, BLK), BLK)
        return ref[rows, pl.ds(pl.multiple_of(g * width, HEAD_SIZE), width)]

    def own(ref, half, c, width):
        g = head_of(c)
        if isinstance(c, int) and c < RKV:
            out = columns(ref, half, 0, width)
            for other in range(1, KVH):
                out = lax.select(g == other, columns(ref, half, other, width), out)
            return out
        out = columns(ref, half, c - RKV, width)
        for other in (c - 1, c):
            out = lax.select(g == other, columns(ref, half, other, width), out)
        return out

    def stage(c, _):
        for half in range(2):
            kv[c, half, 0, 0] = own(k_ref, half, c, HEAD_SIZE)
            kv[c, half, 1, 0] = own(v_ref, half, c, HEAD_SIZE)
        return 0

    def stage_q(h):
        for half in range(2):
            rows = own(q_ref, half, h, ROWS)
            for j in range(GQ):
                qx[0, h, half, j * BLK : (j + 1) * BLK] = rows[:, j * HEAD_SIZE : (j + 1) * HEAD_SIZE]

    for c in range(RKV):
        stage(c, 0)
        stage_q(c)
    lax.fori_loop(RKV, KVH, stage, 0)

    pl.semaphore_wait(barrier, len(near) + 2)

    def first_sends(c):
        push(c, 0, 1, "next")
        push(c, 0, NZ - 1, "far")
        give_sink(c, 0)

    for c in range(LEAD):
        first_sends(c)
    for e in range(1, NX):
        q_copy(e).start()

    tri = lax.rem(lax.broadcasted_iota(jnp.int32, (ROWS, BLK), 0), BLK) >= lax.broadcasted_iota(
        jnp.int32, (ROWS, BLK), 1
    )

    def bias_of(ok):
        return jnp.where(ok, 0.0, NEG).astype(jnp.float32)

    def attend(queries, tiles):
        top, at, places = None, 0, []
        for keys, _, biases in tiles:
            s = dot_nt(queries, keys())
            for i, b in enumerate(biases):
                piece = s[:, i * BLK : (i + 1) * BLK] + b
                s_ref[:, at + i * BLK : at + (i + 1) * BLK] = piece
                top = piece if top is None else jnp.maximum(top, piece)
            places.append((at, len(biases) * BLK))
            at += len(biases) * BLK
        top = jnp.maximum(jnp.max(top, axis=1, keepdims=True), LOW)
        cut = top * CEXP
        total, mixed = None, None
        for (_, values, _), (at, width) in zip(tiles, places):
            w = jnp.exp2(s_ref[:, at : at + width] * CEXP - cut)
            for i in range(width // BLK):
                piece = w[:, i * BLK : (i + 1) * BLK]
                total = piece if total is None else total + piece
            part = jnp.dot(w.astype(jnp.bfloat16), values(), preferred_element_type=jnp.float32)
            mixed = part if mixed is None else mixed + part
        return top, jnp.sum(total, axis=1, keepdims=True), mixed

    def pair(c, half, which, i):
        return lambda: kv[c, half, which, 2 * i : 2 * i + 2].reshape(2 * BLK, HEAD_SIZE)

    def running(c, half):
        k = c - RKV
        up = half == 1
        rows = own(q_ref, half, c, ROWS)
        queries = jnp.concatenate(
            [rows[:, j * HEAD_SIZE : (j + 1) * HEAD_SIZE] for j in range(GQ)], axis=0
        )
        tiles = [(lambda: sink[k, 0], lambda: sink[k, 1], [bias_of(up | (me >= WBLOCKS))])]
        for i in range(NZ // 2):
            biases = [bias_of(up | (me >= d)) for d in (2 * i, 2 * i + 1)]
            if i == 0:
                biases[0] = jnp.where(tri, 0.0, NEG)
            tiles.append((pair(c, half, 0, i), pair(c, half, 1, i), biases))
        _, total, mixed = attend(queries, tiles)
        out = (mixed / total).astype(jnp.bfloat16)
        for j in range(GQ):
            res[c, pl.ds(pl.multiple_of(half * BLK, BLK), BLK), j * HEAD_SIZE : (j + 1) * HEAD_SIZE] = out[
                j * BLK : (j + 1) * BLK
            ]

    def retrieval(h, e):
        qrow = (x + NX - e) % NX
        for half in range(2):
            i_blk = half * nseq + qrow * NZ + z
            i_doc = docs[0, i_blk]
            tiles = []
            for khalf in range(half + 1):
                for i in range(NZ // 2):
                    biases = []
                    for d in (2 * i, 2 * i + 1):
                        j_blk = khalf * nseq + x * NZ + (z + NZ - d) % NZ
                        b = bias_of((docs[0, j_blk] == i_doc) & (j_blk <= i_blk))
                        if d == 0 and khalf == half:
                            b = jnp.where(tri | (j_blk < i_blk), b, NEG)
                        biases.append(b)
                    tiles.append((pair(h, khalf, 0, i), pair(h, khalf, 1, i), biases))
            top, total, mixed = attend(qx[e, h, half], tiles)
            po[e, h, half] = (mixed / jnp.where(total > 0.0, total, 1.0)).astype(jnp.bfloat16)
            for n, column in enumerate((top, total)):
                wide = jnp.broadcast_to(column, (ROWS, BLK))
                for j in range(GQ):
                    row = (half * GQ + j) * 2 + n
                    st[e, h, row : row + 1, :] = wide[j * BLK : (j + 1) * BLK].T[0:1]

        @pl.when(e > 0)
        def _():
            for copy in part_copies(e, h):
                copy.start()

    def combine(h):
        for e in range(1, NX):
            for copy in part_copies(e, h):
                copy.wait_recv()
        for half in range(2):
            for j in range(GQ):
                row = (half * GQ + j) * 2
                tops = [st[0, h, row : row + 1]] + [sr[e, h, row : row + 1] for e in range(NX - 1)]
                sums = [st[0, h, row + 1 : row + 2]] + [sr[e, h, row + 1 : row + 2] for e in range(NX - 1)]
                best = jnp.maximum(jnp.maximum(tops[0], tops[1]), jnp.maximum(tops[2], tops[3]))
                shares = [jnp.exp2((m - best) * CEXP) * l for m, l in zip(tops, sums)]
                whole = shares[0] + shares[1] + shares[2] + shares[3]
                at = slice(j * BLK, (j + 1) * BLK)
                parts = [po[0, h, half, at]] + [pr[e, h, half, at] for e in range(NX - 1)]
                out = None
                for share, part in zip(shares, parts):
                    weight = jnp.broadcast_to(share / whole, (BLK, BLK)).T
                    term = weight * part.astype(jnp.float32)
                    out = term if out is None else out + term
                res[h, half * BLK : (half + 1) * BLK, at] = out.astype(jnp.bfloat16)

    def give_out(k, _):
        place = place_of(k)
        out = res[0]
        for c in (1, jnp.clip(k, RKV, KVH - 1), jnp.clip(k + 1, RKV, KVH - 1), jnp.minimum(k + RKV, KVH - 1)):
            out = lax.select(place == c, res[c], out)
        outst[k] = out
        out_copy(k).start()
        return 0

    def micro(w, _):
        t, u = w // 2, w % 2

        def with_head(c, f):
            @pl.when((c >= 0) & (c < KVH))
            def _():
                f(c)

        @pl.when(u == 0)
        def _():
            with_head(t - 4, lambda c: landed(c, 4))

            def third(c):
                landed(c, 3)

                @pl.when(c < RKV)
                def _():
                    push(c, 3, 4, "next")

                landed(c, 5)

                @pl.when(c >= RKV)
                def _():
                    push(c, 5, 4, "prev")

            with_head(t - 3, third)

        @pl.when(u == 1)
        def _():
            def second(c):
                landed(c, 2)
                push(c, 2, 3, "next")
                landed(c, 6)
                push(c, 6, 5, "prev")

            with_head(t - 2, second)

            def first(c):
                landed(c, 1)
                push(c, 1, 2, "next")
                landed(c, 7)
                push(c, 7, 6, "prev")

            with_head(t - 1, first)
            with_head(t + LEAD, first_sends)

        @pl.when(w == 8)
        def _():
            for e in range(1, NX):
                q_copy(e).wait_recv()

        @pl.when((t >= 4) & (t < 8))
        def _():
            h = (t - 4) // 2
            e = (1 + (w - 8) % 4) % 4
            retrieval(h, e)

        half = 1 - u
        c = t - 4 - half

        @pl.when((c >= RKV) & (c < KVH))
        def _():
            @pl.when(half == 0)
            def _():
                @pl.when(x == 0)
                def _():
                    sink[c - RKV] = kv[c, 0, :, z]

                @pl.when(x > 0)
                def _():
                    sink_copy(c, 0, 1).wait_recv()

            running(c, half)

        @pl.when(w == 17)
        def _():
            lax.fori_loop(0, RKV, lambda h, _: (combine(h), 0)[1], 0)

        @pl.when((u == 0) & (t >= 9))
        def _():
            first = jnp.where(t == 9, 0, t - 7)
            last = jnp.where(t == 12, KVH, t - 6)
            lax.fori_loop(first, last, give_out, 0)

        return 0

    lax.fori_loop(0, 25, micro, 0)

    for k in range(KVH):
        out_copy(k).wait_recv()
        out_copy(k).wait_send()

    def finish(c, _):
        for slot in range(1, NZ):
            for half in range(2):
                block_copy(c, half, slot, half, slot, pos_next).wait_send()
        return 0

    lax.fori_loop(0, KVH, finish, 0)
    for e in range(1, NX):
        q_copy(e).wait_send()
        for h in range(RKV):
            for copy in part_copies(e, h):
                copy.wait_send()

    @pl.when(x == 0)
    def _():
        for c in range(RKV, KVH):
            for r in range(1, NX):
                sink_copy(c, 0, r).wait_send()


def shards(query, keys, values, documents, retrieval_heads):
    rows, width = query.shape[1:]
    bf, f32 = jnp.bfloat16, jnp.float32
    dma = pltpu.SemaphoreType.DMA
    vmem = pl.BlockSpec(memory_space=pltpu.VMEM)
    smem = pl.BlockSpec(memory_space=pltpu.SMEM)
    out = pl.pallas_call(
        kernel,
        out_shape=jax.ShapeDtypeStruct((rows, width), bf),
        in_specs=[smem, smem, vmem, vmem, vmem],
        out_specs=vmem,
        scratch_shapes=[
            pltpu.VMEM((KVH, 2, 2, NZ, BLK, HEAD_SIZE), bf),
            pltpu.VMEM((RUN, 2, BLK, HEAD_SIZE), bf),
            pltpu.VMEM((NX, RKV, 2, ROWS, HEAD_SIZE), bf),
            pltpu.VMEM((NX, RKV, 2, ROWS, HEAD_SIZE), bf),
            pltpu.VMEM((NX - 1, RKV, 2, ROWS, HEAD_SIZE), bf),
            pltpu.VMEM((NX, RKV, 16, BLK), f32),
            pltpu.VMEM((NX - 1, RKV, 16, BLK), f32),
            pltpu.VMEM((KVH, rows, ROWS), bf),
            pltpu.VMEM((KVH, rows, ROWS), bf),
            pltpu.VMEM((ROWS, 2 * NZ * BLK), f32),
            dma((KVH, NZ, 2)),
            dma((KVH, NZ, 2)),
            dma((RUN, NX - 1)),
            dma((RUN,)),
            dma((NX - 1,)),
            dma((NX - 1,)),
            dma((NX - 1, RKV)),
            dma((NX - 1, RKV)),
            dma((NX - 1, RKV)),
            dma((NX - 1, RKV)),
            dma((KVH,)),
            dma((KVH,)),
        ],
        compiler_params=pltpu.CompilerParams(
            collective_id=0, has_side_effects=True, vmem_limit_bytes=50 * 1024 * 1024
        ),
    )(documents, retrieval_heads, query[0], keys[0], values[0])
    return out[None]


def solution(mesh):
    placed = (
        P("section", "seq", None),
        P("section", "seq", None),
        P("section", "seq", None),
        P("section", None),
        P("section", None),
    )
    return jax.shard_map(
        shards, mesh=mesh, in_specs=placed, out_specs=P("section", "seq", None), check_vma=False
    )
```

```python
import math

import jax
import jax.numpy as jnp
from jax import lax
from jax.experimental import pallas as pl
from jax.experimental.pallas import tpu as pltpu
from jax.sharding import PartitionSpec as P

KVH = 8
HEAD_SIZE = 128
RKV = 2
BLK = 128
WBLOCKS = 8
RUN = KVH - RKV
GQ = 3
ROWS = GQ * BLK
NZ = 8
NX = 4
LEAD = 4
PLUS = 3
WAVES = 2 * KVH
LAG = 2
DONE = 1 + 3 * LAG
NEG = -1e30
LOW = -1e29
CEXP = math.log2(math.e) / math.sqrt(HEAD_SIZE)
MESH = pl.DeviceIdType.MESH


def dot_nt(a, b):
    return lax.dot_general(a, b, (((1,), (1,)), ((), ())), preferred_element_type=jnp.float32)


def kernel(
    docs_hbm, heads_hbm, q_hbm, k_hbm, v_hbm, out_ref, docs, heads, q_ref, k_ref, v_ref, isem,
    kv, over, turn, sink, qx, po, pr, pt, st, sr, res, rin, heads_via, heads_in, hsem, s_ref,
    ksend, krecv, vsend, vrecv, usend, urecv, ssend, srecv, qsend, qrecv, wsend, wrecv, psend, precv, tsend, trecv, osend, orecv,
):
    sec = lax.axis_index("section")
    me = lax.axis_index("seq")
    nsec = lax.axis_size("section")
    fetch = [
        pltpu.make_async_copy(src, dst, isem.at[i])
        for i, (src, dst) in enumerate(
            ((heads_hbm, heads), (k_hbm, k_ref), (v_hbm, v_ref), (docs_hbm, docs), (q_hbm, q_ref))
        )
    ]
    for copy in fetch:
        copy.start()
    nseq = NX * NZ
    x, z = me // NZ, me % NZ
    row_next, row_prev = x * NZ + (z + 1) % NZ, x * NZ + (z + NZ - 1) % NZ
    pos_next, pos_prev = (me + 1) % nseq, (me + nseq - 1) % nseq
    pos_far, pos_back = (me + NZ - 1) % nseq, (me + nseq - NZ + 1) % nseq
    row_up, row_down = (me + NZ) % nseq, (me + nseq - NZ) % nseq
    wrap_next = (me + 1) // nseq
    wrap_prev = 1 - (me + nseq - 1) // nseq
    wrap_far = (me + NZ - 1) // nseq

    barrier = pltpu.get_barrier_semaphore()
    near = [row_next, row_prev, pos_next, pos_prev, pos_far, pos_back]
    near += [(x + e) % NX * NZ + z for e in range(1, NX)]
    for to in near:
        pl.semaphore_signal(barrier, inc=1, device_id={"seq": to}, device_id_type=MESH)
    for by in (1, nsec - 1):
        pl.semaphore_signal(
            barrier, inc=1, device_id={"section": (sec + by) % nsec}, device_id_type=MESH
        )

    for copy in fetch[:3]:
        copy.wait()
    lo = jnp.minimum(heads[0, 0], heads[0, 1])
    hi = jnp.maximum(heads[0, 0], heads[0, 1])

    def peer(c, kind):
        ret = c < RKV
        if kind == "next":
            return jnp.where(ret, row_next, pos_next), jnp.where(ret, 0, wrap_next)
        if kind == "prev":
            return jnp.where(ret, row_prev, pos_prev), jnp.where(ret, 0, wrap_prev)
        return jnp.where(ret, row_prev, pos_far), jnp.where(ret, 0, wrap_far)

    def block_copy(c, half, src, dh, dst, to):
        return pltpu.make_async_remote_copy(
            src_ref=kv.at[c, half, :, src], dst_ref=kv.at[c, dh, :, dst],
            send_sem=ksend.at[c, dst, half], recv_sem=krecv.at[c, dst, dh],
            device_id={"seq": to}, device_id_type=MESH,
        )

    def lies(c, slot, half):
        return jnp.where((c >= RKV) & (me < slot), 1 - half, half)

    def push(c, half, src, dst, kind):
        to, swap = peer(c, kind)
        have = lies(c, src, half)
        block_copy(c, have, src, (have + swap) % 2, dst, to).start()

    def landed(c, half, slot):
        have = lies(c, slot, half)
        block_copy(c, have, slot, have, slot, pos_next).wait_recv()
        give_sink(c, half, slot)

    def over_copy(c, half, slot):
        return pltpu.make_async_remote_copy(
            src_ref=kv.at[c, half, :, slot], dst_ref=over.at[c - RKV, half, slot],
            send_sem=ksend.at[c, slot + 1, half], recv_sem=vrecv.at[c - RKV, half, slot],
            device_id={"seq": (me + NZ) % nseq}, device_id_type=MESH,
        )

    def on_copy(c, half, slot):
        swap = (x == 0).astype(jnp.int32)
        dh = (half + swap) % 2
        return pltpu.make_async_remote_copy(
            src_ref=over.at[c - RKV, half, slot], dst_ref=kv.at[c, dh, :, slot + 1],
            send_sem=vsend.at[c - RKV, half, slot], recv_sem=krecv.at[c, slot + 1, dh],
            device_id={"seq": x * NZ}, device_id_type=MESH,
        )

    def push_next(c, half, slot):
        far_end = (z == NZ - 1) & (c >= RKV)

        @pl.when(far_end)
        def _():
            over_copy(c, half, slot).start()

        @pl.when(jnp.logical_not(far_end))
        def _():
            push(c, half, slot, slot + 1, "next")

    def turn_copy(c, half):
        return pltpu.make_async_remote_copy(
            src_ref=kv.at[c, half, :, 0], dst_ref=turn.at[c - RKV, half],
            send_sem=ksend.at[c, NZ - 1, half], recv_sem=urecv.at[c - RKV, half],
            device_id={"seq": pos_prev}, device_id_type=MESH,
        )

    def turn_up(c, half):
        dh = (half + (x == NX - 1).astype(jnp.int32)) % 2
        return pltpu.make_async_remote_copy(
            src_ref=turn.at[c - RKV, half], dst_ref=kv.at[c, dh, :, NZ - 1],
            send_sem=usend.at[c - RKV, half], recv_sem=krecv.at[c, NZ - 1, dh],
            device_id={"seq": row_up}, device_id_type=MESH,
        )

    def turn_round(c, half):
        return pltpu.make_async_remote_copy(
            src_ref=turn.at[c - RKV, half], dst_ref=kv.at[c, half, :, NZ - 2],
            send_sem=ksend.at[c, NZ - 2, half], recv_sem=krecv.at[c, NZ - 2, half],
            device_id={"seq": row_prev}, device_id_type=MESH,
        )

    def pass_turn(c, half):
        @pl.when((c >= RKV) & (z == 0))
        def _():
            turn_copy(c, half).wait_recv()
            turn_up(c, half).start()
            turn_round(c, half).start()

    def pass_over(c, half, slot):
        @pl.when((c >= RKV) & (z == NZ - 1))
        def _():
            over_copy(c, half, slot).wait_recv()
            on_copy(c, half, slot).start()

    def sink_copy(c, slot, r):
        return pltpu.make_async_remote_copy(
            src_ref=kv.at[c, 0, :, slot], dst_ref=sink.at[c - RKV],
            send_sem=ssend.at[c - RKV, r - 1], recv_sem=srecv.at[c - RKV],
            device_id={"seq": r * NZ + z}, device_id_type=MESH,
        )

    def give_sink(c, half, slot):
        @pl.when((x == 0) & (z == slot) & (c >= RKV) & (half == 0))
        def _():
            for r in range(1, NX):
                sink_copy(c, slot, r).start()

    def q_copy(e, h, src):
        back = e == NX - 1 if src == 0 else h == 1
        return pltpu.make_async_remote_copy(
            src_ref=qx.at[src, h], dst_ref=qx.at[e, h], send_sem=qsend.at[e - 1, h], recv_sem=qrecv.at[e - 1, h],
            device_id={"seq": row_down if back else row_up}, device_id_type=MESH,
        )

    def part_copy(e, h):
        return pltpu.make_async_remote_copy(
            src_ref=po.at[e, h], dst_ref=pr.at[e - 1, h],
            send_sem=psend.at[e - 1, h], recv_sem=precv.at[e - 1, h],
            device_id={"seq": (x + NX - e) % NX * NZ + z}, device_id_type=MESH,
        )

    def part_via(h, to):
        return pltpu.make_async_remote_copy(
            src_ref=po.at[2, h], dst_ref=pt.at[h], send_sem=psend.at[1, h], recv_sem=wrecv.at[h],
            device_id={"seq": to}, device_id_type=MESH,
        )

    def part_on(h, to):
        return pltpu.make_async_remote_copy(
            src_ref=pt.at[h], dst_ref=pr.at[1, h], send_sem=wsend.at[h], recv_sem=precv.at[1, h],
            device_id={"seq": to}, device_id_type=MESH,
        )

    def stat_copy(e, h):
        return pltpu.make_async_remote_copy(
            src_ref=st.at[e, h], dst_ref=sr.at[e - 1, h],
            send_sem=tsend.at[e - 1, h], recv_sem=trecv.at[e - 1, h],
            device_id={"seq": (x + NX - e) % NX * NZ + z}, device_id_type=MESH,
        )

    def out_copy(c):
        return pltpu.make_async_remote_copy(
            src_ref=res.at[c], dst_ref=rin.at[c], send_sem=osend.at[c], recv_sem=orecv.at[c],
            device_id={"section": (sec + 1) % nsec}, device_id_type=MESH,
        )

    def heads_copy():
        return pltpu.make_async_remote_copy(
            src_ref=heads_hbm, dst_ref=heads_via, send_sem=hsem.at[0], recv_sem=hsem.at[1],
            device_id={"section": (sec + 1) % nsec}, device_id_type=MESH,
        )

    def heads_in_copy():
        return pltpu.make_async_copy(heads_via, heads_in, hsem.at[2])

    def head_of(c):
        k = c - RKV
        g = k + (k >= lo).astype(jnp.int32)
        g = g + (g >= hi).astype(jnp.int32)
        return jnp.where(c == 0, heads[0, 0], jnp.where(c == 1, heads[0, 1], g))

    def place_of(g):
        first, second = heads_in[0, 0], heads_in[0, 1]
        low, high = jnp.minimum(first, second), jnp.maximum(first, second)
        run = RKV + g - (g > low).astype(jnp.int32) - (g > high).astype(jnp.int32)
        return jnp.where(g == first, 0, jnp.where(g == second, 1, run))

    def columns(ref, half, g, width):
        rows = pl.ds(pl.multiple_of(half * BLK, BLK), BLK)
        return ref[rows, pl.ds(pl.multiple_of(g * width, HEAD_SIZE), width)]

    def own(ref, half, c, width):
        g = head_of(c)
        if isinstance(c, int) and c < RKV:
            out = columns(ref, half, 0, width)
            for other in range(1, KVH):
                out = lax.select(g == other, columns(ref, half, other, width), out)
            return out
        out = columns(ref, half, c - RKV, width)
        for other in (c - 1, c):
            out = lax.select(g == other, columns(ref, half, other, width), out)
        return out

    def stage(c, _):
        for half in range(2):
            kv[c, half, 0, 0] = own(k_ref, half, c, HEAD_SIZE)
            kv[c, half, 1, 0] = own(v_ref, half, c, HEAD_SIZE)
        return 0

    def stage_q(h):
        for half in range(2):
            rows = own(q_ref, half, h, ROWS)
            for j in range(GQ):
                qx[0, h, half, j * BLK : (j + 1) * BLK] = rows[:, j * HEAD_SIZE : (j + 1) * HEAD_SIZE]

    for c in range(RKV):
        stage(c, 0)
    pl.semaphore_wait(barrier, len(near) + 2)

    def first_sends(c, half):
        push_next(c, half, 0)
        turns = (z == 1) & (c >= RKV)

        @pl.when(turns)
        def _():
            turn_copy(c, half).start()

        @pl.when(jnp.logical_not(turns))
        def _():
            push(c, half, 0, NZ - 1, "far")

        give_sink(c, half, 0)

    for n in range(LEAD):
        first_sends(jnp.int32(n // 2), n % 2)
    for copy in fetch[3:]:
        copy.wait()
    for c in range(RKV):
        stage_q(c)
    for h in range(RKV):
        for e in (1, NX - 1):
            q_copy(e, h, 0).start()
    heads_copy().start()
    lax.fori_loop(RKV, KVH, stage, 0)

    tri = lax.rem(lax.broadcasted_iota(jnp.int32, (ROWS, BLK), 0), BLK) >= lax.broadcasted_iota(
        jnp.int32, (ROWS, BLK), 1
    )

    def bias_of(ok):
        return jnp.where(ok, 0.0, NEG).astype(jnp.float32)

    def attend(queries, tiles):
        top, at, places = None, 0, []
        for keys, _, biases in tiles:
            s = dot_nt(queries, keys())
            for i, b in enumerate(biases):
                piece = s[:, i * BLK : (i + 1) * BLK] + b
                s_ref[:, at + i * BLK : at + (i + 1) * BLK] = piece
                top = piece if top is None else jnp.maximum(top, piece)
            places.append((at, len(biases) * BLK))
            at += len(biases) * BLK
        top = jnp.maximum(jnp.max(top, axis=1, keepdims=True), LOW)
        cut = top * CEXP
        total, mixed = None, None
        for (_, values, _), (at, width) in zip(tiles, places):
            w = jnp.exp2(s_ref[:, at : at + width] * CEXP - cut)
            for i in range(width // BLK):
                piece = w[:, i * BLK : (i + 1) * BLK]
                total = piece if total is None else total + piece
            part = jnp.dot(w.astype(jnp.bfloat16), values(), preferred_element_type=jnp.float32)
            mixed = part if mixed is None else mixed + part
        return top, jnp.sum(total, axis=1, keepdims=True), mixed

    def pair(c, half, which, i):
        return lambda: kv[c, half, which, 2 * i : 2 * i + 2].reshape(2 * BLK, HEAD_SIZE)

    def running(c, half):
        k = c - RKV
        up = half == 1
        rows = own(q_ref, half, c, ROWS)
        queries = jnp.concatenate(
            [rows[:, j * HEAD_SIZE : (j + 1) * HEAD_SIZE] for j in range(GQ)], axis=0
        )
        tiles = [(lambda: sink[k, 0], lambda: sink[k, 1], [bias_of(up | (me >= WBLOCKS))])]
        for i in range(NZ // 2):
            biases = [bias_of(up | (me >= d)) for d in (2 * i, 2 * i + 1)]
            if i == 0:
                biases[0] = jnp.where(tri, 0.0, NEG)
            tiles.append((pair(c, half, 0, i), pair(c, half, 1, i), biases))
        _, total, mixed = attend(queries, tiles)
        out = (mixed / total).astype(jnp.bfloat16)
        for j in range(GQ):
            res[c, pl.ds(pl.multiple_of(half * BLK, BLK), BLK), j * HEAD_SIZE : (j + 1) * HEAD_SIZE] = out[
                j * BLK : (j + 1) * BLK
            ]

    def retrieval(h, e):
        qrow = (x + NX - e) % NX
        for half in range(2):
            i_blk = half * nseq + qrow * NZ + z
            i_doc = docs[0, i_blk]
            tiles = []
            for khalf in range(half + 1):
                for i in range(NZ // 2):
                    biases = []
                    for d in (2 * i, 2 * i + 1):
                        j_blk = khalf * nseq + x * NZ + (z + NZ - d) % NZ
                        b = bias_of((docs[0, j_blk] == i_doc) & (j_blk <= i_blk))
                        if d == 0 and khalf == half:
                            b = jnp.where(tri | (j_blk < i_blk), b, NEG)
                        biases.append(b)
                    tiles.append((pair(h, khalf, 0, i), pair(h, khalf, 1, i), biases))
            top, total, mixed = attend(qx[e, h, half], tiles)
            po[e, h, half] = (mixed / jnp.where(total > 0.0, total, 1.0)).astype(jnp.bfloat16)
            for n, column in enumerate((top, total)):
                wide = jnp.broadcast_to(column, (ROWS, BLK))
                for j in range(GQ):
                    row = (half * GQ + j) * 2 + n
                    st[e, h, row : row + 1, :] = wide[j * BLK : (j + 1) * BLK].T[0:1]

        @pl.when(e > 0)
        def _():
            stat_copy(e, h).start()

        @pl.when((e > 0) & (e != 2))
        def _():
            part_copy(e, h).start()

        @pl.when(e == 2)
        def _():
            part_via(h, jnp.where(h == 0, row_up, row_down)).start()

    def combine(h):
        for e in range(1, NX):
            part_copy(e, h).wait_recv()
            stat_copy(e, h).wait_recv()
        for half in range(2):
            for j in range(GQ):
                row = (half * GQ + j) * 2
                tops = [st[0, h, row : row + 1]] + [sr[e, h, row : row + 1] for e in range(NX - 1)]
                sums = [st[0, h, row + 1 : row + 2]] + [sr[e, h, row + 1 : row + 2] for e in range(NX - 1)]
                best = jnp.maximum(jnp.maximum(tops[0], tops[1]), jnp.maximum(tops[2], tops[3]))
                shares = [jnp.exp2((m - best) * CEXP) * l for m, l in zip(tops, sums)]
                whole = shares[0] + shares[1] + shares[2] + shares[3]
                at = slice(j * BLK, (j + 1) * BLK)
                parts = [po[0, h, half, at]] + [pr[e, h, half, at] for e in range(NX - 1)]
                out = None
                for share, part in zip(shares, parts):
                    weight = jnp.broadcast_to(share / whole, (BLK, BLK)).T
                    term = weight * part.astype(jnp.float32)
                    out = term if out is None else out + term
                res[h, half * BLK : (half + 1) * BLK, at] = out.astype(jnp.bfloat16)
        out_copy(h).start()

    def place(g):
        at = place_of(g)
        out = rin[0]
        for c in sorted({1, max(g, RKV), max(g + 1, RKV), min(g + RKV, KVH - 1)} - {KVH}):
            out = lax.select(at == c, rin[c], out)
        out_ref[:, g * ROWS : (g + 1) * ROWS] = out

    def micro(w, _):
        def with_wave(n, f):
            @pl.when((n >= 0) & (n < WAVES))
            def _():
                f(n // 2, n % 2)

        with_wave(w - DONE, lambda c, half: landed(c, half, 4))

        def third(c, half):
            landed(c, half, 3)

            @pl.when(c < PLUS)
            def _():
                push(c, half, 3, 4, "next")

            landed(c, half, 5)

            @pl.when(c >= PLUS)
            def _():
                push(c, half, 5, 4, "prev")

        with_wave(w - 1 - 2 * LAG, third)

        def second(c, half):
            landed(c, half, 2)
            push(c, half, 2, 3, "next")
            landed(c, half, 6)
            push(c, half, 6, 5, "prev")

        with_wave(w - 1 - LAG, second)

        def first(c, half):
            landed(c, half, 1)
            push_next(c, half, 1)
            landed(c, half, 7)

            @pl.when((z > 0) | (c < RKV))
            def _():
                push(c, half, 7, 6, "prev")


        with_wave(w + LEAD - 2, pass_turn)
        with_wave(w + LEAD - 2, lambda c, half: pass_over(c, half, 0))
        with_wave(w - 2, lambda c, half: pass_over(c, half, 1))
        with_wave(w - 1, first)
        with_wave(w + LEAD, first_sends)

        @pl.when(w == 1)
        def _():
            q_copy(1, 0, 0).wait_recv()
            q_copy(2, 0, 1).start()
            q_copy(NX - 1, 1, 0).wait_recv()
            q_copy(2, 1, NX - 1).start()

        @pl.when((w == DONE + 5) | (w == DONE + 9))
        def _():
            h = (w - DONE - 5) // NX
            part_via(h, row_up).wait_recv()
            part_on(h, jnp.where(h == 0, row_up, row_down)).start()

        @pl.when(w == DONE + 2)
        def _():
            for h in range(RKV):
                q_copy(2, h, 0).wait_recv()
                q_copy(NX - 1 if h == 0 else 1, h, 0).wait_recv()

        @pl.when((w >= DONE + 2) & (w < DONE + 10))
        def _():
            retrieval((w - DONE - 2) // NX, (w - DONE - 1) % NX)

        half = (w + NZ - DONE - 1) % 2
        c = (w + NZ - DONE - 1) // 2 - NZ // 2

        @pl.when((c >= RKV) & (c < KVH))
        def _():
            @pl.when(half == 0)
            def _():
                @pl.when(x == 0)
                def _():
                    sink[c - RKV] = kv[c, 0, :, z]

                @pl.when(x > 0)
                def _():
                    sink_copy(c, 0, 1).wait_recv()

            running(c, half)

            @pl.when(half == 1)
            def _():
                out_copy(c).start()

        @pl.when(w == DONE + 11)
        def _():
            lax.fori_loop(0, RKV, lambda h, _: (combine(h), 0)[1], 0)

        @pl.when(w == DONE + 14)
        def _():
            heads_copy().wait_recv()
            heads_in_copy().start()
            heads_in_copy().wait()
            for c in range(KVH - 2):
                out_copy(c).wait_recv()
            for g in range(KVH - 4):
                place(g)

        return 0

    lax.fori_loop(0, DONE + WAVES + 1, micro, 0)

    for c in range(KVH - 2, KVH):
        out_copy(c).wait_recv()
    for g in range(KVH - 4, KVH):
        place(g)
    for c in range(KVH):
        out_copy(c).wait_send()
    heads_copy().wait_send()

    def finish(c, _):
        for slot in range(1, NZ):
            for half in range(2):
                block_copy(c, half, slot, half, slot, pos_next).wait_send()
        return 0

    lax.fori_loop(0, KVH, finish, 0)
    for e in range(1, NX):
        for h in range(RKV):
            q_copy(e, h, 0).wait_send()
        for h in range(RKV):
            part_copy(e, h).wait_send()
            stat_copy(e, h).wait_send()
    for h in range(RKV):
        part_on(h, row_up).wait_send()

    @pl.when(z == 0)
    def _():
        for c in range(RKV, KVH):
            for half in range(2):
                turn_up(c, half).wait_send()

    @pl.when(z == NZ - 1)
    def _():
        for c in range(RKV, KVH):
            for half in range(2):
                for slot in range(2):
                    on_copy(c, half, slot).wait_send()

    @pl.when(x == 0)
    def _():
        for c in range(RKV, KVH):
            for r in range(1, NX):
                sink_copy(c, 0, r).wait_send()


def shards(query, keys, values, documents, retrieval_heads):
    rows, width = query.shape[1:]
    bf, f32 = jnp.bfloat16, jnp.float32
    dma = pltpu.SemaphoreType.DMA
    vmem = pl.BlockSpec(memory_space=pltpu.VMEM)
    hbm = pl.BlockSpec(memory_space=pltpu.HBM)
    out = pl.pallas_call(
        kernel,
        out_shape=jax.ShapeDtypeStruct((rows, width), bf),
        in_specs=[hbm] * 5,
        out_specs=vmem,
        scratch_shapes=[
            pltpu.SMEM(documents.shape, jnp.int32),
            pltpu.SMEM(retrieval_heads.shape, jnp.int32),
            pltpu.VMEM((rows, width), bf),
            pltpu.VMEM(keys.shape[1:], bf),
            pltpu.VMEM(values.shape[1:], bf),
            dma((5,)),
            pltpu.VMEM((KVH, 2, 2, NZ, BLK, HEAD_SIZE), bf),
            pltpu.VMEM((RUN, 2, 2, 2, BLK, HEAD_SIZE), bf),
            pltpu.VMEM((RUN, 2, 2, BLK, HEAD_SIZE), bf),
            pltpu.VMEM((RUN, 2, BLK, HEAD_SIZE), bf),
            pltpu.VMEM((NX, RKV, 2, ROWS, HEAD_SIZE), bf),
            pltpu.VMEM((NX, RKV, 2, ROWS, HEAD_SIZE), bf),
            pltpu.VMEM((NX - 1, RKV, 2, ROWS, HEAD_SIZE), bf),
            pltpu.VMEM((RKV, 2, ROWS, HEAD_SIZE), bf),
            pltpu.VMEM((NX, RKV, 16, BLK), f32),
            pltpu.VMEM((NX - 1, RKV, 16, BLK), f32),
            pltpu.VMEM((KVH, rows, ROWS), bf),
            pltpu.VMEM((KVH, rows, ROWS), bf),
            pltpu.VMEM(retrieval_heads.shape, jnp.int32),
            pltpu.SMEM(retrieval_heads.shape, jnp.int32),
            dma((3,)),
            pltpu.VMEM((ROWS, 2 * NZ * BLK), f32),
            dma((KVH, NZ, 2)),
            dma((KVH, NZ, 2)),
            dma((RUN, 2, 2)),
            dma((RUN, 2, 2)),
            dma((RUN, 2)),
            dma((RUN, 2)),
            dma((RUN, NX - 1)),
            dma((RUN,)),
            dma((NX - 1, RKV)),
            dma((NX - 1, RKV)),
            dma((RKV,)),
            dma((RKV,)),
            dma((NX - 1, RKV)),
            dma((NX - 1, RKV)),
            dma((NX - 1, RKV)),
            dma((NX - 1, RKV)),
            dma((KVH,)),
            dma((KVH,)),
        ],
        compiler_params=pltpu.CompilerParams(
            collective_id=0, has_side_effects=True, vmem_limit_bytes=56 * 1024 * 1024
        ),
    )(documents, retrieval_heads, query[0], keys[0], values[0])
    return out[None]


def solution(mesh):
    placed = (
        P("section", "seq", None),
        P("section", "seq", None),
        P("section", "seq", None),
        P("section", None),
        P("section", None),
    )
    return jax.shard_map(
        shards, mesh=mesh, in_specs=placed, out_specs=P("section", "seq", None), check_vma=False
    )
```

```python
import math

import jax
import jax.numpy as jnp
from jax import lax
from jax.experimental import pallas as pl
from jax.experimental.pallas import tpu as pltpu
from jax.sharding import PartitionSpec as P

KVH = 8
HEAD_SIZE = 128
RKV = 2
BLK = 128
WBLOCKS = 8
RUN = KVH - RKV
GQ = 3
ROWS = GQ * BLK
NZ = 8
NX = 4
LEAD = 4
PLUS = 5
WAVES = 2 * KVH
LAG = 2
DONE = 1 + 3 * LAG
NEG = -1e30
LOW = -1e29
CEXP = math.log2(math.e) / math.sqrt(HEAD_SIZE)
MESH = pl.DeviceIdType.MESH


def dot_nt(a, b):
    return lax.dot_general(a, b, (((1,), (1,)), ((), ())), preferred_element_type=jnp.float32)


def kernel(
    docs_hbm, heads_hbm, q_hbm, k_hbm, v_hbm, out_ref, docs, heads, q_ref, k_ref, v_ref, isem,
    kv, over, turn, sink, qx, po, pr, pt, st, sr, res, rin, heads_via, heads_in, hsem, s_ref,
    ksend, krecv, vsend, vrecv, usend, urecv, ssend, srecv, qsend, qrecv, wsend, wrecv, psend, precv, tsend, trecv, osend, orecv,
):
    sec = lax.axis_index("section")
    me = lax.axis_index("seq")
    nsec = lax.axis_size("section")
    fetch = [
        pltpu.make_async_copy(src, dst, isem.at[i])
        for i, (src, dst) in enumerate(
            ((heads_hbm, heads), (k_hbm, k_ref), (v_hbm, v_ref), (docs_hbm, docs), (q_hbm, q_ref))
        )
    ]
    for copy in fetch:
        copy.start()
    nseq = NX * NZ
    x, z = me // NZ, me % NZ
    row_next, row_prev = x * NZ + (z + 1) % NZ, x * NZ + (z + NZ - 1) % NZ
    pos_next, pos_prev = (me + 1) % nseq, (me + nseq - 1) % nseq
    pos_far, pos_back = (me + NZ - 1) % nseq, (me + nseq - NZ + 1) % nseq
    row_up, row_down = (me + NZ) % nseq, (me + nseq - NZ) % nseq
    wrap_next = (me + 1) // nseq
    wrap_prev = 1 - (me + nseq - 1) // nseq
    wrap_far = (me + NZ - 1) // nseq

    barrier = pltpu.get_barrier_semaphore()
    near = [row_next, row_prev, pos_next, pos_prev, pos_far, pos_back]
    near += [(x + e) % NX * NZ + z for e in range(1, NX)]
    for to in near:
        pl.semaphore_signal(barrier, inc=1, device_id={"seq": to}, device_id_type=MESH)
    for by in (1, nsec - 1):
        pl.semaphore_signal(
            barrier, inc=1, device_id={"section": (sec + by) % nsec}, device_id_type=MESH
        )

    for copy in fetch[:3]:
        copy.wait()
    lo = jnp.minimum(heads[0, 0], heads[0, 1])
    hi = jnp.maximum(heads[0, 0], heads[0, 1])

    def peer(c, kind):
        ret = c < RKV
        if kind == "next":
            return jnp.where(ret, row_next, pos_next), jnp.where(ret, 0, wrap_next)
        if kind == "prev":
            return jnp.where(ret, row_prev, pos_prev), jnp.where(ret, 0, wrap_prev)
        return jnp.where(ret, row_prev, pos_far), jnp.where(ret, 0, wrap_far)

    def block_copy(c, half, src, dh, dst, to):
        return pltpu.make_async_remote_copy(
            src_ref=kv.at[c, half, :, src], dst_ref=kv.at[c, dh, :, dst],
            send_sem=ksend.at[c, dst, half], recv_sem=krecv.at[c, dst, dh],
            device_id={"seq": to}, device_id_type=MESH,
        )

    def lies(c, slot, half):
        return jnp.where((c >= RKV) & (me < slot), 1 - half, half)

    def push(c, half, src, dst, kind):
        to, swap = peer(c, kind)
        have = lies(c, src, half)
        block_copy(c, have, src, (have + swap) % 2, dst, to).start()

    def landed(c, half, slot):
        have = lies(c, slot, half)
        block_copy(c, have, slot, have, slot, pos_next).wait_recv()
        give_sink(c, half, slot)

    def over_copy(c, half, slot):
        return pltpu.make_async_remote_copy(
            src_ref=kv.at[c, half, :, slot], dst_ref=over.at[c - RKV, half, slot],
            send_sem=ksend.at[c, slot + 1, half], recv_sem=vrecv.at[c - RKV, half, slot],
            device_id={"seq": (me + NZ) % nseq}, device_id_type=MESH,
        )

    def on_copy(c, half, slot):
        swap = (x == 0).astype(jnp.int32)
        dh = (half + swap) % 2
        return pltpu.make_async_remote_copy(
            src_ref=over.at[c - RKV, half, slot], dst_ref=kv.at[c, dh, :, slot + 1],
            send_sem=vsend.at[c - RKV, half, slot], recv_sem=krecv.at[c, slot + 1, dh],
            device_id={"seq": x * NZ}, device_id_type=MESH,
        )

    def push_next(c, half, slot):
        far_end = (z == NZ - 1) & (c >= RKV)

        @pl.when(far_end)
        def _():
            over_copy(c, half, slot).start()

        @pl.when(jnp.logical_not(far_end))
        def _():
            push(c, half, slot, slot + 1, "next")

    def turn_copy(c, half):
        return pltpu.make_async_remote_copy(
            src_ref=kv.at[c, half, :, 0], dst_ref=turn.at[c - RKV, half],
            send_sem=ksend.at[c, NZ - 1, half], recv_sem=urecv.at[c - RKV, half],
            device_id={"seq": pos_prev}, device_id_type=MESH,
        )

    def turn_up(c, half):
        dh = (half + (x == NX - 1).astype(jnp.int32)) % 2
        return pltpu.make_async_remote_copy(
            src_ref=turn.at[c - RKV, half], dst_ref=kv.at[c, dh, :, NZ - 1],
            send_sem=usend.at[c - RKV, half], recv_sem=krecv.at[c, NZ - 1, dh],
            device_id={"seq": row_up}, device_id_type=MESH,
        )

    def turn_round(c, half):
        return pltpu.make_async_remote_copy(
            src_ref=turn.at[c - RKV, half], dst_ref=kv.at[c, half, :, NZ - 2],
            send_sem=ksend.at[c, NZ - 2, half], recv_sem=krecv.at[c, NZ - 2, half],
            device_id={"seq": row_prev}, device_id_type=MESH,
        )

    def pass_turn(c, half):
        @pl.when((c >= RKV) & (z == 0))
        def _():
            turn_copy(c, half).wait_recv()
            turn_up(c, half).start()
            turn_round(c, half).start()

    def pass_over(c, half, slot):
        @pl.when((c >= RKV) & (z == NZ - 1))
        def _():
            over_copy(c, half, slot).wait_recv()
            on_copy(c, half, slot).start()

    def sink_copy(c, slot, r):
        return pltpu.make_async_remote_copy(
            src_ref=kv.at[c, 0, :, slot], dst_ref=sink.at[c - RKV],
            send_sem=ssend.at[c - RKV, r - 1], recv_sem=srecv.at[c - RKV],
            device_id={"seq": r * NZ + z}, device_id_type=MESH,
        )

    def give_sink(c, half, slot):
        @pl.when((x == 0) & (z == slot) & (c >= RKV) & (half == 0))
        def _():
            for r in range(1, NX):
                sink_copy(c, slot, r).start()

    def q_copy(e, h):
        return pltpu.make_async_remote_copy(
            src_ref=qx.at[0, h], dst_ref=qx.at[e, h], send_sem=qsend.at[e - 1, h], recv_sem=qrecv.at[e - 1, h],
            device_id={"seq": row_up if e == 1 else row_down}, device_id_type=MESH,
        )

    def goes_back(h):
        return (z == 0) | (h == 1)

    def q_from(h):
        return jnp.where(goes_back(h), NX - 1, 1)

    def q_on(h):
        return pltpu.make_async_remote_copy(
            src_ref=qx.at[q_from(h), h], dst_ref=qx.at[2, h], send_sem=qsend.at[1, h], recv_sem=qrecv.at[1, h],
            device_id={"seq": jnp.where(goes_back(h), row_down, row_up)}, device_id_type=MESH,
        )

    def q_wait(e, h):
        pltpu.make_async_remote_copy(
            src_ref=qx.at[e, h], dst_ref=qx.at[e, h], send_sem=qsend.at[e - 1, h], recv_sem=qrecv.at[e - 1, h],
            device_id={"seq": row_up}, device_id_type=MESH,
        ).wait_recv()

    def part_copy(e, h):
        return pltpu.make_async_remote_copy(
            src_ref=po.at[e, h], dst_ref=pr.at[e - 1, h],
            send_sem=psend.at[e - 1, h], recv_sem=precv.at[e - 1, h],
            device_id={"seq": (x + NX - e) % NX * NZ + z}, device_id_type=MESH,
        )

    def part_via(h, to):
        return pltpu.make_async_remote_copy(
            src_ref=po.at[2, h], dst_ref=pt.at[h], send_sem=psend.at[1, h], recv_sem=wrecv.at[h],
            device_id={"seq": to}, device_id_type=MESH,
        )

    def part_on(h, to):
        return pltpu.make_async_remote_copy(
            src_ref=pt.at[h], dst_ref=pr.at[1, h], send_sem=wsend.at[h], recv_sem=precv.at[1, h],
            device_id={"seq": to}, device_id_type=MESH,
        )

    def stat_copy(e, h):
        return pltpu.make_async_remote_copy(
            src_ref=st.at[e, h], dst_ref=sr.at[e - 1, h],
            send_sem=tsend.at[e - 1, h], recv_sem=trecv.at[e - 1, h],
            device_id={"seq": (x + NX - e) % NX * NZ + z}, device_id_type=MESH,
        )

    def out_copy(c):
        return pltpu.make_async_remote_copy(
            src_ref=res.at[c], dst_ref=rin.at[c], send_sem=osend.at[c], recv_sem=orecv.at[c],
            device_id={"section": (sec + 1) % nsec}, device_id_type=MESH,
        )

    def heads_copy():
        return pltpu.make_async_remote_copy(
            src_ref=heads_hbm, dst_ref=heads_via, send_sem=hsem.at[0], recv_sem=hsem.at[1],
            device_id={"section": (sec + 1) % nsec}, device_id_type=MESH,
        )

    def heads_in_copy():
        return pltpu.make_async_copy(heads_via, heads_in, hsem.at[2])

    def head_of(c):
        k = c - RKV
        g = k + (k >= lo).astype(jnp.int32)
        g = g + (g >= hi).astype(jnp.int32)
        return jnp.where(c == 0, heads[0, 0], jnp.where(c == 1, heads[0, 1], g))

    def place_of(g):
        first, second = heads_in[0, 0], heads_in[0, 1]
        low, high = jnp.minimum(first, second), jnp.maximum(first, second)
        run = RKV + g - (g > low).astype(jnp.int32) - (g > high).astype(jnp.int32)
        return jnp.where(g == first, 0, jnp.where(g == second, 1, run))

    def columns(ref, half, g, width):
        rows = pl.ds(pl.multiple_of(half * BLK, BLK), BLK)
        return ref[rows, pl.ds(pl.multiple_of(g * width, HEAD_SIZE), width)]

    def own(ref, half, c, width):
        g = head_of(c)
        if isinstance(c, int) and c < RKV:
            out = columns(ref, half, 0, width)
            for other in range(1, KVH):
                out = lax.select(g == other, columns(ref, half, other, width), out)
            return out
        out = columns(ref, half, c - RKV, width)
        for other in (c - 1, c):
            out = lax.select(g == other, columns(ref, half, other, width), out)
        return out

    def stage(c, _):
        for half in range(2):
            kv[c, half, 0, 0] = own(k_ref, half, c, HEAD_SIZE)
            kv[c, half, 1, 0] = own(v_ref, half, c, HEAD_SIZE)
        return 0

    def stage_q(h):
        for half in range(2):
            rows = own(q_ref, half, h, ROWS)
            for j in range(GQ):
                qx[0, h, half, j * BLK : (j + 1) * BLK] = rows[:, j * HEAD_SIZE : (j + 1) * HEAD_SIZE]

    for c in range(RKV):
        stage(c, 0)
    pl.semaphore_wait(barrier, len(near) + 2)

    def first_sends(c, half):
        push_next(c, half, 0)
        turns = (z == 1) & (c >= RKV)

        @pl.when(turns)
        def _():
            turn_copy(c, half).start()

        @pl.when(jnp.logical_not(turns))
        def _():
            push(c, half, 0, NZ - 1, "far")

        give_sink(c, half, 0)

    for n in range(LEAD):
        first_sends(jnp.int32(n // 2), n % 2)
    for copy in fetch[3:]:
        copy.wait()
    for c in range(RKV):
        stage_q(c)
    for h in range(RKV):
        for e in (1, NX - 1):
            q_copy(e, h).start()
    heads_copy().start()
    lax.fori_loop(RKV, KVH, stage, 0)

    tri = lax.rem(lax.broadcasted_iota(jnp.int32, (ROWS, BLK), 0), BLK) >= lax.broadcasted_iota(
        jnp.int32, (ROWS, BLK), 1
    )

    def bias_of(ok):
        return jnp.where(ok, 0.0, NEG).astype(jnp.float32)

    def attend(queries, tiles):
        top, at, places = None, 0, []
        for keys, _, biases in tiles:
            s = dot_nt(queries, keys())
            for i, b in enumerate(biases):
                piece = s[:, i * BLK : (i + 1) * BLK] + b
                s_ref[:, at + i * BLK : at + (i + 1) * BLK] = piece
                top = piece if top is None else jnp.maximum(top, piece)
            places.append((at, len(biases) * BLK))
            at += len(biases) * BLK
        top = jnp.maximum(jnp.max(top, axis=1, keepdims=True), LOW)
        cut = top * CEXP
        total, mixed = None, None
        for (_, values, _), (at, width) in zip(tiles, places):
            w = jnp.exp2(s_ref[:, at : at + width] * CEXP - cut)
            for i in range(width // BLK):
                piece = w[:, i * BLK : (i + 1) * BLK]
                total = piece if total is None else total + piece
            part = jnp.dot(w.astype(jnp.bfloat16), values(), preferred_element_type=jnp.float32)
            mixed = part if mixed is None else mixed + part
        return top, jnp.sum(total, axis=1, keepdims=True), mixed

    def pair(c, half, which, i):
        return lambda: kv[c, half, which, 2 * i : 2 * i + 2].reshape(2 * BLK, HEAD_SIZE)

    def running(c, half):
        k = c - RKV
        up = half == 1
        rows = own(q_ref, half, c, ROWS)
        queries = jnp.concatenate(
            [rows[:, j * HEAD_SIZE : (j + 1) * HEAD_SIZE] for j in range(GQ)], axis=0
        )
        tiles = [(lambda: sink[k, 0], lambda: sink[k, 1], [bias_of(up | (me >= WBLOCKS))])]
        for i in range(NZ // 2):
            biases = [bias_of(up | (me >= d)) for d in (2 * i, 2 * i + 1)]
            if i == 0:
                biases[0] = jnp.where(tri, 0.0, NEG)
            tiles.append((pair(c, half, 0, i), pair(c, half, 1, i), biases))
        _, total, mixed = attend(queries, tiles)
        out = (mixed / total).astype(jnp.bfloat16)
        for j in range(GQ):
            res[c, pl.ds(pl.multiple_of(half * BLK, BLK), BLK), j * HEAD_SIZE : (j + 1) * HEAD_SIZE] = out[
                j * BLK : (j + 1) * BLK
            ]

    def retrieval(h, e):
        qrow = (x + NX - e) % NX
        for half in range(2):
            i_blk = half * nseq + qrow * NZ + z
            i_doc = docs[0, i_blk]
            tiles = []
            for khalf in range(half + 1):
                for i in range(NZ // 2):
                    biases = []
                    for d in (2 * i, 2 * i + 1):
                        j_blk = khalf * nseq + x * NZ + (z + NZ - d) % NZ
                        b = bias_of((docs[0, j_blk] == i_doc) & (j_blk <= i_blk))
                        if d == 0 and khalf == half:
                            b = jnp.where(tri | (j_blk < i_blk), b, NEG)
                        biases.append(b)
                    tiles.append((pair(h, khalf, 0, i), pair(h, khalf, 1, i), biases))
            top, total, mixed = attend(qx[e, h, half], tiles)
            po[e, h, half] = (mixed / jnp.where(total > 0.0, total, 1.0)).astype(jnp.bfloat16)
            for n, column in enumerate((top, total)):
                wide = jnp.broadcast_to(column, (ROWS, BLK))
                for j in range(GQ):
                    row = (half * GQ + j) * 2 + n
                    st[e, h, row : row + 1, :] = wide[j * BLK : (j + 1) * BLK].T[0:1]

        @pl.when(e > 0)
        def _():
            stat_copy(e, h).start()

        @pl.when((e > 0) & (e != 2))
        def _():
            part_copy(e, h).start()

        @pl.when(e == 2)
        def _():
            part_via(h, jnp.where(goes_back(h), row_down, row_up)).start()

    def combine(h):
        for e in range(1, NX):
            part_copy(e, h).wait_recv()
            stat_copy(e, h).wait_recv()
        for half in range(2):
            for j in range(GQ):
                row = (half * GQ + j) * 2
                tops = [st[0, h, row : row + 1]] + [sr[e, h, row : row + 1] for e in range(NX - 1)]
                sums = [st[0, h, row + 1 : row + 2]] + [sr[e, h, row + 1 : row + 2] for e in range(NX - 1)]
                best = jnp.maximum(jnp.maximum(tops[0], tops[1]), jnp.maximum(tops[2], tops[3]))
                shares = [jnp.exp2((m - best) * CEXP) * l for m, l in zip(tops, sums)]
                whole = shares[0] + shares[1] + shares[2] + shares[3]
                at = slice(j * BLK, (j + 1) * BLK)
                parts = [po[0, h, half, at]] + [pr[e, h, half, at] for e in range(NX - 1)]
                out = None
                for share, part in zip(shares, parts):
                    weight = jnp.broadcast_to(share / whole, (BLK, BLK)).T
                    term = weight * part.astype(jnp.float32)
                    out = term if out is None else out + term
                res[h, half * BLK : (half + 1) * BLK, at] = out.astype(jnp.bfloat16)
        out_copy(h).start()

    def place(g):
        at = place_of(g)
        out = rin[0]
        for c in sorted({1, max(g, RKV), max(g + 1, RKV), min(g + RKV, KVH - 1)} - {KVH}):
            out = lax.select(at == c, rin[c], out)
        out_ref[:, g * ROWS : (g + 1) * ROWS] = out

    def micro(w, _):
        def with_wave(n, f):
            @pl.when((n >= 0) & (n < WAVES))
            def _():
                f(n // 2, n % 2)

        with_wave(w - DONE, lambda c, half: landed(c, half, 4))

        def third(c, half):
            landed(c, half, 3)

            @pl.when(c < PLUS)
            def _():
                push(c, half, 3, 4, "next")

            landed(c, half, 5)

            @pl.when(c >= PLUS)
            def _():
                push(c, half, 5, 4, "prev")

        with_wave(w - 1 - 2 * LAG, third)

        def second(c, half):
            landed(c, half, 2)
            push(c, half, 2, 3, "next")
            landed(c, half, 6)
            push(c, half, 6, 5, "prev")

        with_wave(w - 1 - LAG, second)

        def first(c, half):
            landed(c, half, 1)
            push_next(c, half, 1)
            landed(c, half, 7)

            @pl.when((z > 0) | (c < RKV))
            def _():
                push(c, half, 7, 6, "prev")


        with_wave(w + LEAD - 2, pass_turn)
        with_wave(w + LEAD - 2, lambda c, half: pass_over(c, half, 0))
        with_wave(w - 2, lambda c, half: pass_over(c, half, 1))
        with_wave(w - 1, first)
        with_wave(w + LEAD, first_sends)

        @pl.when(w == 1)
        def _():
            for h in range(RKV):
                q_wait(q_from(h), h)
                q_on(h).start()

        @pl.when((w == DONE + 5) | (w == DONE + 9))
        def _():
            h = (w - DONE - 5) // NX
            part_via(h, row_up).wait_recv()
            part_on(h, jnp.where(goes_back(h), row_down, row_up)).start()

        @pl.when(w == DONE + 2)
        def _():
            for h in range(RKV):
                q_wait(2, h)
                q_wait(NX - q_from(h), h)

        @pl.when((w >= DONE + 2) & (w < DONE + 10))
        def _():
            retrieval((w - DONE - 2) // NX, (w - DONE - 1) % NX)

        half = (w + NZ - DONE - 1) % 2
        c = (w + NZ - DONE - 1) // 2 - NZ // 2

        @pl.when((c >= RKV) & (c < KVH))
        def _():
            @pl.when(half == 0)
            def _():
                @pl.when(x == 0)
                def _():
                    sink[c - RKV] = kv[c, 0, :, z]

                @pl.when(x > 0)
                def _():
                    sink_copy(c, 0, 1).wait_recv()

            running(c, half)

            @pl.when(half == 1)
            def _():
                out_copy(c).start()

        @pl.when(w == DONE + 11)
        def _():
            lax.fori_loop(0, RKV, lambda h, _: (combine(h), 0)[1], 0)

        @pl.when(w == DONE + 14)
        def _():
            heads_copy().wait_recv()
            heads_in_copy().start()
            heads_in_copy().wait()
            for c in range(KVH - 2):
                out_copy(c).wait_recv()
            for g in range(KVH - 4):
                place(g)

        return 0

    lax.fori_loop(0, DONE + WAVES + 1, micro, 0)

    for c in range(KVH - 2, KVH):
        out_copy(c).wait_recv()
    for g in range(KVH - 4, KVH):
        place(g)
    for c in range(KVH):
        out_copy(c).wait_send()
    heads_copy().wait_send()

    def finish(c, _):
        for slot in range(1, NZ):
            for half in range(2):
                block_copy(c, half, slot, half, slot, pos_next).wait_send()
        return 0

    lax.fori_loop(0, KVH, finish, 0)
    for e in range(1, NX):
        for h in range(RKV):
            q_copy(e, h).wait_send()
        for h in range(RKV):
            part_copy(e, h).wait_send()
            stat_copy(e, h).wait_send()
    for h in range(RKV):
        part_on(h, row_up).wait_send()

    @pl.when(z == 0)
    def _():
        for c in range(RKV, KVH):
            for half in range(2):
                turn_up(c, half).wait_send()

    @pl.when(z == NZ - 1)
    def _():
        for c in range(RKV, KVH):
            for half in range(2):
                for slot in range(2):
                    on_copy(c, half, slot).wait_send()

    @pl.when(x == 0)
    def _():
        for c in range(RKV, KVH):
            for r in range(1, NX):
                sink_copy(c, 0, r).wait_send()


def shards(query, keys, values, documents, retrieval_heads):
    rows, width = query.shape[1:]
    bf, f32 = jnp.bfloat16, jnp.float32
    dma = pltpu.SemaphoreType.DMA
    vmem = pl.BlockSpec(memory_space=pltpu.VMEM)
    hbm = pl.BlockSpec(memory_space=pltpu.HBM)
    out = pl.pallas_call(
        kernel,
        out_shape=jax.ShapeDtypeStruct((rows, width), bf),
        in_specs=[hbm] * 5,
        out_specs=vmem,
        scratch_shapes=[
            pltpu.SMEM(documents.shape, jnp.int32),
            pltpu.SMEM(retrieval_heads.shape, jnp.int32),
            pltpu.VMEM((rows, width), bf),
            pltpu.VMEM(keys.shape[1:], bf),
            pltpu.VMEM(values.shape[1:], bf),
            dma((5,)),
            pltpu.VMEM((KVH, 2, 2, NZ, BLK, HEAD_SIZE), bf),
            pltpu.VMEM((RUN, 2, 2, 2, BLK, HEAD_SIZE), bf),
            pltpu.VMEM((RUN, 2, 2, BLK, HEAD_SIZE), bf),
            pltpu.VMEM((RUN, 2, BLK, HEAD_SIZE), bf),
            pltpu.VMEM((NX, RKV, 2, ROWS, HEAD_SIZE), bf),
            pltpu.VMEM((NX, RKV, 2, ROWS, HEAD_SIZE), bf),
            pltpu.VMEM((NX - 1, RKV, 2, ROWS, HEAD_SIZE), bf),
            pltpu.VMEM((RKV, 2, ROWS, HEAD_SIZE), bf),
            pltpu.VMEM((NX, RKV, 16, BLK), f32),
            pltpu.VMEM((NX - 1, RKV, 16, BLK), f32),
            pltpu.VMEM((KVH, rows, ROWS), bf),
            pltpu.VMEM((KVH, rows, ROWS), bf),
            pltpu.VMEM(retrieval_heads.shape, jnp.int32),
            pltpu.SMEM(retrieval_heads.shape, jnp.int32),
            dma((3,)),
            pltpu.VMEM((ROWS, 2 * NZ * BLK), f32),
            dma((KVH, NZ, 2)),
            dma((KVH, NZ, 2)),
            dma((RUN, 2, 2)),
            dma((RUN, 2, 2)),
            dma((RUN, 2)),
            dma((RUN, 2)),
            dma((RUN, NX - 1)),
            dma((RUN,)),
            dma((NX - 1, RKV)),
            dma((NX - 1, RKV)),
            dma((RKV,)),
            dma((RKV,)),
            dma((NX - 1, RKV)),
            dma((NX - 1, RKV)),
            dma((NX - 1, RKV)),
            dma((NX - 1, RKV)),
            dma((KVH,)),
            dma((KVH,)),
        ],
        compiler_params=pltpu.CompilerParams(
            collective_id=0, has_side_effects=True, vmem_limit_bytes=56 * 1024 * 1024
        ),
    )(documents, retrieval_heads, query[0], keys[0], values[0])
    return out[None]


def solution(mesh):
    placed = (
        P("section", "seq", None),
        P("section", "seq", None),
        P("section", "seq", None),
        P("section", None),
        P("section", None),
    )
    return jax.shard_map(
        shards, mesh=mesh, in_specs=placed, out_specs=P("section", "seq", None), check_vma=False
    )
```

```python
import math

import jax
import jax.numpy as jnp
from jax import lax
from jax.experimental import pallas as pl
from jax.experimental.pallas import tpu as pltpu
from jax.sharding import PartitionSpec as P

KVH = 8
HEAD_SIZE = 128
RKV = 2
BLK = 128
WBLOCKS = 8
RUN = KVH - RKV
GQ = 3
ROWS = GQ * BLK
NZ = 8
NX = 4
LEAD = 4
WAVES = 2 * KVH
LAG = 2
DONE = 1 + 3 * LAG
NEG = -1e30
LOW = -1e29
CEXP = math.log2(math.e) / math.sqrt(HEAD_SIZE)
MESH = pl.DeviceIdType.MESH


def dot_nt(a, b):
    return lax.dot_general(a, b, (((1,), (1,)), ((), ())), preferred_element_type=jnp.float32)


def kernel(
    docs_hbm, heads_hbm, q_hbm, k_hbm, v_hbm, out_ref, docs, heads, q_ref, k_ref, v_ref, isem,
    kv, over, turn, sink, qx, po, pr, pt, st, sr, res, rin, heads_via, heads_in, hsem, s_ref,
    ksend, krecv, vsend, vrecv, usend, urecv, ssend, srecv, qsend, qrecv, wsend, wrecv, psend, precv, tsend, trecv, osend, orecv,
):
    sec = lax.axis_index("section")
    me = lax.axis_index("seq")
    nsec = lax.axis_size("section")
    fetch = [
        pltpu.make_async_copy(src, dst, isem.at[i])
        for i, (src, dst) in enumerate(
            ((heads_hbm, heads), (k_hbm, k_ref), (v_hbm, v_ref), (docs_hbm, docs), (q_hbm, q_ref))
        )
    ]
    for copy in fetch:
        copy.start()
    nseq = NX * NZ
    x, z = me // NZ, me % NZ
    row_next, row_prev = x * NZ + (z + 1) % NZ, x * NZ + (z + NZ - 1) % NZ
    pos_next, pos_prev = (me + 1) % nseq, (me + nseq - 1) % nseq
    pos_far, pos_back = (me + NZ - 1) % nseq, (me + nseq - NZ + 1) % nseq
    row_up, row_down = (me + NZ) % nseq, (me + nseq - NZ) % nseq
    wrap_next = (me + 1) // nseq
    wrap_prev = 1 - (me + nseq - 1) // nseq
    wrap_far = (me + NZ - 1) // nseq

    barrier = pltpu.get_barrier_semaphore()
    near = [row_next, row_prev, pos_next, pos_prev, pos_far, pos_back]
    near += [(x + e) % NX * NZ + z for e in range(1, NX)]
    for to in near:
        pl.semaphore_signal(barrier, inc=1, device_id={"seq": to}, device_id_type=MESH)
    for by in (1, nsec - 1):
        pl.semaphore_signal(
            barrier, inc=1, device_id={"section": (sec + by) % nsec}, device_id_type=MESH
        )

    for copy in fetch[:3]:
        copy.wait()
    lo = jnp.minimum(heads[0, 0], heads[0, 1])
    hi = jnp.maximum(heads[0, 0], heads[0, 1])

    def peer(c, kind):
        ret = c < RKV
        if kind == "next":
            return jnp.where(ret, row_next, pos_next), jnp.where(ret, 0, wrap_next)
        if kind == "prev":
            return jnp.where(ret, row_prev, pos_prev), jnp.where(ret, 0, wrap_prev)
        return jnp.where(ret, row_prev, pos_far), jnp.where(ret, 0, wrap_far)

    def block_copy(c, half, src, dh, dst, to):
        return pltpu.make_async_remote_copy(
            src_ref=kv.at[c, half, :, src], dst_ref=kv.at[c, dh, :, dst],
            send_sem=ksend.at[c, dst, half], recv_sem=krecv.at[c, dst, dh],
            device_id={"seq": to}, device_id_type=MESH,
        )

    def lies(c, slot, half):
        return jnp.where((c >= RKV) & (me < slot), 1 - half, half)

    def push(c, half, src, dst, kind):
        to, swap = peer(c, kind)
        have = lies(c, src, half)
        block_copy(c, have, src, (have + swap) % 2, dst, to).start()

    def landed(c, half, slot):
        have = lies(c, slot, half)
        block_copy(c, have, slot, have, slot, pos_next).wait_recv()
        give_sink(c, half, slot)

    def over_copy(c, half, slot):
        return pltpu.make_async_remote_copy(
            src_ref=kv.at[c, half, :, slot], dst_ref=over.at[c - RKV, half, slot],
            send_sem=ksend.at[c, slot + 1, half], recv_sem=vrecv.at[c - RKV, half, slot],
            device_id={"seq": (me + NZ) % nseq}, device_id_type=MESH,
        )

    def on_copy(c, half, slot):
        swap = (x == 0).astype(jnp.int32)
        dh = (half + swap) % 2
        return pltpu.make_async_remote_copy(
            src_ref=over.at[c - RKV, half, slot], dst_ref=kv.at[c, dh, :, slot + 1],
            send_sem=vsend.at[c - RKV, half, slot], recv_sem=krecv.at[c, slot + 1, dh],
            device_id={"seq": x * NZ}, device_id_type=MESH,
        )

    def push_next(c, half, slot):
        far_end = (z == NZ - 1) & (c >= RKV)

        @pl.when(far_end)
        def _():
            over_copy(c, half, slot).start()

        @pl.when(jnp.logical_not(far_end))
        def _():
            push(c, half, slot, slot + 1, "next")

    def turn_copy(c, half):
        return pltpu.make_async_remote_copy(
            src_ref=kv.at[c, half, :, 0], dst_ref=turn.at[c - RKV, half],
            send_sem=ksend.at[c, NZ - 1, half], recv_sem=urecv.at[c - RKV, half],
            device_id={"seq": pos_prev}, device_id_type=MESH,
        )

    def turn_up(c, half):
        dh = (half + (x == NX - 1).astype(jnp.int32)) % 2
        return pltpu.make_async_remote_copy(
            src_ref=turn.at[c - RKV, half], dst_ref=kv.at[c, dh, :, NZ - 1],
            send_sem=usend.at[c - RKV, half], recv_sem=krecv.at[c, NZ - 1, dh],
            device_id={"seq": row_up}, device_id_type=MESH,
        )

    def turn_round(c, half):
        return pltpu.make_async_remote_copy(
            src_ref=turn.at[c - RKV, half], dst_ref=kv.at[c, half, :, NZ - 2],
            send_sem=ksend.at[c, NZ - 2, half], recv_sem=krecv.at[c, NZ - 2, half],
            device_id={"seq": row_prev}, device_id_type=MESH,
        )

    def pass_turn(c, half):
        @pl.when((c >= RKV) & (z == 0))
        def _():
            turn_copy(c, half).wait_recv()
            turn_up(c, half).start()
            turn_round(c, half).start()

    def pass_over(c, half, slot):
        @pl.when((c >= RKV) & (z == NZ - 1))
        def _():
            over_copy(c, half, slot).wait_recv()
            on_copy(c, half, slot).start()

    def sink_copy(c, slot, r):
        return pltpu.make_async_remote_copy(
            src_ref=kv.at[c, 0, :, slot], dst_ref=sink.at[c - RKV],
            send_sem=ssend.at[c - RKV, r - 1], recv_sem=srecv.at[c - RKV],
            device_id={"seq": r * NZ + z}, device_id_type=MESH,
        )

    def give_sink(c, half, slot):
        @pl.when((x == 0) & (z == slot) & (c >= RKV) & (half == 0))
        def _():
            for r in range(1, NX):
                sink_copy(c, slot, r).start()

    def q_copy(e, h):
        return pltpu.make_async_remote_copy(
            src_ref=qx.at[0, h], dst_ref=qx.at[e, h], send_sem=qsend.at[e - 1, h], recv_sem=qrecv.at[e - 1, h],
            device_id={"seq": row_up if e == 1 else row_down}, device_id_type=MESH,
        )

    def goes_on(c):
        return (c < RKV) | (c % 2 == 0)

    def goes_back(h):
        return (z == 0) | (h == 1)

    def q_from(h):
        return jnp.where(goes_back(h), NX - 1, 1)

    def q_on(h):
        return pltpu.make_async_remote_copy(
            src_ref=qx.at[q_from(h), h], dst_ref=qx.at[2, h], send_sem=qsend.at[1, h], recv_sem=qrecv.at[1, h],
            device_id={"seq": jnp.where(goes_back(h), row_down, row_up)}, device_id_type=MESH,
        )

    def q_wait(e, h):
        pltpu.make_async_remote_copy(
            src_ref=qx.at[e, h], dst_ref=qx.at[e, h], send_sem=qsend.at[e - 1, h], recv_sem=qrecv.at[e - 1, h],
            device_id={"seq": row_up}, device_id_type=MESH,
        ).wait_recv()

    def part_copy(e, h):
        return pltpu.make_async_remote_copy(
            src_ref=po.at[e, h], dst_ref=pr.at[e - 1, h],
            send_sem=psend.at[e - 1, h], recv_sem=precv.at[e - 1, h],
            device_id={"seq": (x + NX - e) % NX * NZ + z}, device_id_type=MESH,
        )

    def part_via(h, to):
        return pltpu.make_async_remote_copy(
            src_ref=po.at[2, h], dst_ref=pt.at[h], send_sem=psend.at[1, h], recv_sem=wrecv.at[h],
            device_id={"seq": to}, device_id_type=MESH,
        )

    def part_on(h, to):
        return pltpu.make_async_remote_copy(
            src_ref=pt.at[h], dst_ref=pr.at[1, h], send_sem=wsend.at[h], recv_sem=precv.at[1, h],
            device_id={"seq": to}, device_id_type=MESH,
        )

    def stat_copy(e, h):
        return pltpu.make_async_remote_copy(
            src_ref=st.at[e, h], dst_ref=sr.at[e - 1, h],
            send_sem=tsend.at[e - 1, h], recv_sem=trecv.at[e - 1, h],
            device_id={"seq": (x + NX - e) % NX * NZ + z}, device_id_type=MESH,
        )

    def out_copy(c):
        return pltpu.make_async_remote_copy(
            src_ref=res.at[c], dst_ref=rin.at[c], send_sem=osend.at[c], recv_sem=orecv.at[c],
            device_id={"section": (sec + 1) % nsec}, device_id_type=MESH,
        )

    def heads_copy():
        return pltpu.make_async_remote_copy(
            src_ref=heads_hbm, dst_ref=heads_via, send_sem=hsem.at[0], recv_sem=hsem.at[1],
            device_id={"section": (sec + 1) % nsec}, device_id_type=MESH,
        )

    def heads_in_copy():
        return pltpu.make_async_copy(heads_via, heads_in, hsem.at[2])

    def head_of(c):
        k = c - RKV
        g = k + (k >= lo).astype(jnp.int32)
        g = g + (g >= hi).astype(jnp.int32)
        return jnp.where(c == 0, heads[0, 0], jnp.where(c == 1, heads[0, 1], g))

    def place_of(g):
        first, second = heads_in[0, 0], heads_in[0, 1]
        low, high = jnp.minimum(first, second), jnp.maximum(first, second)
        run = RKV + g - (g > low).astype(jnp.int32) - (g > high).astype(jnp.int32)
        return jnp.where(g == first, 0, jnp.where(g == second, 1, run))

    def columns(ref, half, g, width):
        rows = pl.ds(pl.multiple_of(half * BLK, BLK), BLK)
        return ref[rows, pl.ds(pl.multiple_of(g * width, HEAD_SIZE), width)]

    def own(ref, half, c, width):
        g = head_of(c)
        if isinstance(c, int) and c < RKV:
            out = columns(ref, half, 0, width)
            for other in range(1, KVH):
                out = lax.select(g == other, columns(ref, half, other, width), out)
            return out
        out = columns(ref, half, c - RKV, width)
        for other in (c - 1, c):
            out = lax.select(g == other, columns(ref, half, other, width), out)
        return out

    def stage(c, _):
        for half in range(2):
            kv[c, half, 0, 0] = own(k_ref, half, c, HEAD_SIZE)
            kv[c, half, 1, 0] = own(v_ref, half, c, HEAD_SIZE)
        return 0

    def stage_q(h):
        for half in range(2):
            rows = own(q_ref, half, h, ROWS)
            for j in range(GQ):
                qx[0, h, half, j * BLK : (j + 1) * BLK] = rows[:, j * HEAD_SIZE : (j + 1) * HEAD_SIZE]

    for c in range(RKV):
        stage(c, 0)
    pl.semaphore_wait(barrier, len(near) + 2)

    def first_sends(c, half):
        push_next(c, half, 0)
        turns = (z == 1) & (c >= RKV)

        @pl.when(turns)
        def _():
            turn_copy(c, half).start()

        @pl.when(jnp.logical_not(turns))
        def _():
            push(c, half, 0, NZ - 1, "far")

        give_sink(c, half, 0)

    for n in range(LEAD):
        first_sends(jnp.int32(n // 2), n % 2)
    for copy in fetch[3:]:
        copy.wait()
    for c in range(RKV):
        stage_q(c)
    for h in range(RKV):
        for e in (1, NX - 1):
            q_copy(e, h).start()
    heads_copy().start()
    lax.fori_loop(RKV, KVH, stage, 0)

    tri = lax.rem(lax.broadcasted_iota(jnp.int32, (ROWS, BLK), 0), BLK) >= lax.broadcasted_iota(
        jnp.int32, (ROWS, BLK), 1
    )

    def bias_of(ok):
        return jnp.where(ok, 0.0, NEG).astype(jnp.float32)

    def attend(queries, tiles):
        top, at, places = None, 0, []
        for keys, _, biases in tiles:
            s = dot_nt(queries, keys())
            for i, b in enumerate(biases):
                piece = s[:, i * BLK : (i + 1) * BLK] + b
                s_ref[:, at + i * BLK : at + (i + 1) * BLK] = piece
                top = piece if top is None else jnp.maximum(top, piece)
            places.append((at, len(biases) * BLK))
            at += len(biases) * BLK
        top = jnp.maximum(jnp.max(top, axis=1, keepdims=True), LOW)
        cut = top * CEXP
        total, mixed = None, None
        for (_, values, _), (at, width) in zip(tiles, places):
            w = jnp.exp2(s_ref[:, at : at + width] * CEXP - cut)
            for i in range(width // BLK):
                piece = w[:, i * BLK : (i + 1) * BLK]
                total = piece if total is None else total + piece
            part = jnp.dot(w.astype(jnp.bfloat16), values(), preferred_element_type=jnp.float32)
            mixed = part if mixed is None else mixed + part
        return top, jnp.sum(total, axis=1, keepdims=True), mixed

    def pair(c, half, which, i):
        return lambda: kv[c, half, which, 2 * i : 2 * i + 2].reshape(2 * BLK, HEAD_SIZE)

    def running(c, half):
        k = c - RKV
        up = half == 1
        rows = own(q_ref, half, c, ROWS)
        queries = jnp.concatenate(
            [rows[:, j * HEAD_SIZE : (j + 1) * HEAD_SIZE] for j in range(GQ)], axis=0
        )
        tiles = [(lambda: sink[k, 0], lambda: sink[k, 1], [bias_of(up | (me >= WBLOCKS))])]
        for i in range(NZ // 2):
            biases = [bias_of(up | (me >= d)) for d in (2 * i, 2 * i + 1)]
            if i == 0:
                biases[0] = jnp.where(tri, 0.0, NEG)
            tiles.append((pair(c, half, 0, i), pair(c, half, 1, i), biases))
        _, total, mixed = attend(queries, tiles)
        out = (mixed / total).astype(jnp.bfloat16)
        for j in range(GQ):
            res[c, pl.ds(pl.multiple_of(half * BLK, BLK), BLK), j * HEAD_SIZE : (j + 1) * HEAD_SIZE] = out[
                j * BLK : (j + 1) * BLK
            ]

    def retrieval(h, e):
        qrow = (x + NX - e) % NX
        for half in range(2):
            i_blk = half * nseq + qrow * NZ + z
            i_doc = docs[0, i_blk]
            tiles = []
            for khalf in range(half + 1):
                for i in range(NZ // 2):
                    biases = []
                    for d in (2 * i, 2 * i + 1):
                        j_blk = khalf * nseq + x * NZ + (z + NZ - d) % NZ
                        b = bias_of((docs[0, j_blk] == i_doc) & (j_blk <= i_blk))
                        if d == 0 and khalf == half:
                            b = jnp.where(tri | (j_blk < i_blk), b, NEG)
                        biases.append(b)
                    tiles.append((pair(h, khalf, 0, i), pair(h, khalf, 1, i), biases))
            top, total, mixed = attend(qx[e, h, half], tiles)
            po[e, h, half] = (mixed / jnp.where(total > 0.0, total, 1.0)).astype(jnp.bfloat16)
            for n, column in enumerate((top, total)):
                wide = jnp.broadcast_to(column, (ROWS, BLK))
                for j in range(GQ):
                    row = (half * GQ + j) * 2 + n
                    st[e, h, row : row + 1, :] = wide[j * BLK : (j + 1) * BLK].T[0:1]

        @pl.when(e > 0)
        def _():
            stat_copy(e, h).start()

        @pl.when((e > 0) & (e != 2))
        def _():
            part_copy(e, h).start()

        @pl.when(e == 2)
        def _():
            part_via(h, jnp.where(goes_back(h), row_down, row_up)).start()

    def combine(h):
        for e in range(1, NX):
            part_copy(e, h).wait_recv()
            stat_copy(e, h).wait_recv()
        for half in range(2):
            for j in range(GQ):
                row = (half * GQ + j) * 2
                tops = [st[0, h, row : row + 1]] + [sr[e, h, row : row + 1] for e in range(NX - 1)]
                sums = [st[0, h, row + 1 : row + 2]] + [sr[e, h, row + 1 : row + 2] for e in range(NX - 1)]
                best = jnp.maximum(jnp.maximum(tops[0], tops[1]), jnp.maximum(tops[2], tops[3]))
                shares = [jnp.exp2((m - best) * CEXP) * l for m, l in zip(tops, sums)]
                whole = shares[0] + shares[1] + shares[2] + shares[3]
                at = slice(j * BLK, (j + 1) * BLK)
                parts = [po[0, h, half, at]] + [pr[e, h, half, at] for e in range(NX - 1)]
                out = None
                for share, part in zip(shares, parts):
                    weight = jnp.broadcast_to(share / whole, (BLK, BLK)).T
                    term = weight * part.astype(jnp.float32)
                    out = term if out is None else out + term
                res[h, half * BLK : (half + 1) * BLK, at] = out.astype(jnp.bfloat16)
        out_copy(h).start()

    def place(g):
        at = place_of(g)
        out = rin[0]
        for c in sorted({1, max(g, RKV), max(g + 1, RKV), min(g + RKV, KVH - 1)} - {KVH}):
            out = lax.select(at == c, rin[c], out)
        out_ref[:, g * ROWS : (g + 1) * ROWS] = out

    def micro(w, _):
        def with_wave(n, f):
            @pl.when((n >= 0) & (n < WAVES))
            def _():
                f(n // 2, n % 2)

        with_wave(w - DONE, lambda c, half: landed(c, half, 4))

        def third(c, half):
            landed(c, half, 3)

            @pl.when(goes_on(c))
            def _():
                push(c, half, 3, 4, "next")

            landed(c, half, 5)

            @pl.when(jnp.logical_not(goes_on(c)))
            def _():
                push(c, half, 5, 4, "prev")

        with_wave(w - 1 - 2 * LAG, third)

        def second(c, half):
            landed(c, half, 2)
            push(c, half, 2, 3, "next")
            landed(c, half, 6)
            push(c, half, 6, 5, "prev")

        with_wave(w - 1 - LAG, second)

        def first(c, half):
            landed(c, half, 1)
            push_next(c, half, 1)
            landed(c, half, 7)

            @pl.when((z > 0) | (c < RKV))
            def _():
                push(c, half, 7, 6, "prev")


        with_wave(w + LEAD - 2, pass_turn)
        with_wave(w + LEAD - 2, lambda c, half: pass_over(c, half, 0))
        with_wave(w - 2, lambda c, half: pass_over(c, half, 1))
        with_wave(w - 1, first)
        with_wave(w + LEAD, first_sends)

        @pl.when(w == 1)
        def _():
            for h in range(RKV):
                q_wait(q_from(h), h)
                q_on(h).start()

        @pl.when((w == DONE + 5) | (w == DONE + 9))
        def _():
            h = (w - DONE - 5) // NX
            part_via(h, row_up).wait_recv()
            part_on(h, jnp.where(goes_back(h), row_down, row_up)).start()

        @pl.when(w == DONE + 2)
        def _():
            for h in range(RKV):
                q_wait(2, h)
                q_wait(NX - q_from(h), h)

        @pl.when((w >= DONE + 2) & (w < DONE + 10))
        def _():
            retrieval((w - DONE - 2) // NX, (w - DONE - 1) % NX)

        half = (w + NZ - DONE - 1) % 2
        c = (w + NZ - DONE - 1) // 2 - NZ // 2

        @pl.when((c >= RKV) & (c < KVH))
        def _():
            @pl.when(half == 0)
            def _():
                @pl.when(x == 0)
                def _():
                    sink[c - RKV] = kv[c, 0, :, z]

                @pl.when(x > 0)
                def _():
                    sink_copy(c, 0, 1).wait_recv()

            running(c, half)

            @pl.when(half == 1)
            def _():
                out_copy(c).start()

        @pl.when(w == DONE + 11)
        def _():
            lax.fori_loop(0, RKV, lambda h, _: (combine(h), 0)[1], 0)

        @pl.when(w == DONE + 14)
        def _():
            heads_copy().wait_recv()
            heads_in_copy().start()
            heads_in_copy().wait()
            for c in range(KVH - 2):
                out_copy(c).wait_recv()
            for g in range(KVH - 4):
                place(g)

        return 0

    lax.fori_loop(0, DONE + WAVES + 1, micro, 0)

    for c in range(KVH - 2, KVH):
        out_copy(c).wait_recv()
    for g in range(KVH - 4, KVH):
        place(g)
    for c in range(KVH):
        out_copy(c).wait_send()
    heads_copy().wait_send()

    def finish(c, _):
        for slot in range(1, NZ):
            for half in range(2):
                block_copy(c, half, slot, half, slot, pos_next).wait_send()
        return 0

    lax.fori_loop(0, KVH, finish, 0)
    for e in range(1, NX):
        for h in range(RKV):
            q_copy(e, h).wait_send()
        for h in range(RKV):
            part_copy(e, h).wait_send()
            stat_copy(e, h).wait_send()
    for h in range(RKV):
        part_on(h, row_up).wait_send()

    @pl.when(z == 0)
    def _():
        for c in range(RKV, KVH):
            for half in range(2):
                turn_up(c, half).wait_send()

    @pl.when(z == NZ - 1)
    def _():
        for c in range(RKV, KVH):
            for half in range(2):
                for slot in range(2):
                    on_copy(c, half, slot).wait_send()

    @pl.when(x == 0)
    def _():
        for c in range(RKV, KVH):
            for r in range(1, NX):
                sink_copy(c, 0, r).wait_send()


def shards(query, keys, values, documents, retrieval_heads):
    rows, width = query.shape[1:]
    bf, f32 = jnp.bfloat16, jnp.float32
    dma = pltpu.SemaphoreType.DMA
    vmem = pl.BlockSpec(memory_space=pltpu.VMEM)
    hbm = pl.BlockSpec(memory_space=pltpu.HBM)
    out = pl.pallas_call(
        kernel,
        out_shape=jax.ShapeDtypeStruct((rows, width), bf),
        in_specs=[hbm] * 5,
        out_specs=vmem,
        scratch_shapes=[
            pltpu.SMEM(documents.shape, jnp.int32),
            pltpu.SMEM(retrieval_heads.shape, jnp.int32),
            pltpu.VMEM((rows, width), bf),
            pltpu.VMEM(keys.shape[1:], bf),
            pltpu.VMEM(values.shape[1:], bf),
            dma((5,)),
            pltpu.VMEM((KVH, 2, 2, NZ, BLK, HEAD_SIZE), bf),
            pltpu.VMEM((RUN, 2, 2, 2, BLK, HEAD_SIZE), bf),
            pltpu.VMEM((RUN, 2, 2, BLK, HEAD_SIZE), bf),
            pltpu.VMEM((RUN, 2, BLK, HEAD_SIZE), bf),
            pltpu.VMEM((NX, RKV, 2, ROWS, HEAD_SIZE), bf),
            pltpu.VMEM((NX, RKV, 2, ROWS, HEAD_SIZE), bf),
            pltpu.VMEM((NX - 1, RKV, 2, ROWS, HEAD_SIZE), bf),
            pltpu.VMEM((RKV, 2, ROWS, HEAD_SIZE), bf),
            pltpu.VMEM((NX, RKV, 16, BLK), f32),
            pltpu.VMEM((NX - 1, RKV, 16, BLK), f32),
            pltpu.VMEM((KVH, rows, ROWS), bf),
            pltpu.VMEM((KVH, rows, ROWS), bf),
            pltpu.VMEM(retrieval_heads.shape, jnp.int32),
            pltpu.SMEM(retrieval_heads.shape, jnp.int32),
            dma((3,)),
            pltpu.VMEM((ROWS, 2 * NZ * BLK), f32),
            dma((KVH, NZ, 2)),
            dma((KVH, NZ, 2)),
            dma((RUN, 2, 2)),
            dma((RUN, 2, 2)),
            dma((RUN, 2)),
            dma((RUN, 2)),
            dma((RUN, NX - 1)),
            dma((RUN,)),
            dma((NX - 1, RKV)),
            dma((NX - 1, RKV)),
            dma((RKV,)),
            dma((RKV,)),
            dma((NX - 1, RKV)),
            dma((NX - 1, RKV)),
            dma((NX - 1, RKV)),
            dma((NX - 1, RKV)),
            dma((KVH,)),
            dma((KVH,)),
        ],
        compiler_params=pltpu.CompilerParams(
            collective_id=0, has_side_effects=True, vmem_limit_bytes=56 * 1024 * 1024
        ),
    )(documents, retrieval_heads, query[0], keys[0], values[0])
    return out[None]


def solution(mesh):
    placed = (
        P("section", "seq", None),
        P("section", "seq", None),
        P("section", "seq", None),
        P("section", None),
        P("section", None),
    )
    return jax.shard_map(
        shards, mesh=mesh, in_specs=placed, out_specs=P("section", "seq", None), check_vma=False
    )
```
